512 devices in a mesh: inp: 64 (over y_hi, z, core), tm: 8 (over y_lo, x).
Axes of the slice: x: 4, y: 4 (y_hi: 2, y_lo: 2; y = y_hi * 2 + y_lo), z: 16, core: 2. Of those that a mesh axis runs over, the one named last changes fastest.
Arguments:
- samples: bfloat16 [2048, 65536], P('inp', 'tm'), may hold values from -6 to 6
- tail: bfloat16 [2048, 6144], P('inp'), may hold values from -6 to 6
- taps: float32 [4, 2048], replicated, may hold values from -3 to 3
- tile_table: int32 [64, 4], P('inp'), may hold values from 0 to 3, as said below
Outputs:
- visibilities: float32 [64, 4, 2, 32, 32, 1024], P('inp', None, None, None, None, 'tm')
The draws below stay inside these ranges and needn't reach their ends.
Inputs may be any that keep to these rules, and one draw needn't show every extreme that they name: `tile_table`: each row holds 4 distinct offsets; offsets 0 and 3 both occur.
All inputs are finite; a program needn't handle non-finite values.
Results may differ from the reference program's by a relative error of at most 0.0064.
Values may be sent and summed in bfloat16 or wider, within the bound.
No kernel may reach another device: no remote copies, remote signals or barrier semaphores. Data moves between devices by JAX's collectives and lax.ppermute only.
A program may use at most 64 MiB of HBM per device.

```python
import math
import jax
import jax.numpy as jnp
from jax import lax

F = 1024
L = 2048
TAPS = 4
A_DEV = 32
SPAN = 4
TILES_DEV = 4
NBLK = 64
A = 2048
SPEC = 32
NT = 65536


def draw_tile_table(key, part):
    scores = jax.random.randint(key, (NBLK, SPAN), 0, 1 << 20) * SPAN + jnp.arange(SPAN, dtype=jnp.int32)[None, :]
    scores = scores.at[0, SPAN - 1].set(-1)
    scores = scores.at[1, 0].set(-1)
    ordering = jnp.argsort(scores, axis=1, stable=True)
    return ordering[:, :TILES_DEV].astype(jnp.int32)


def levels(own_key, shape, split, smallest, high):
    gain = 1.0
    for position, blocks in split:
        draws = jax.random.uniform(jax.random.fold_in(jax.random.fold_in(own_key, 6), position), (blocks,), jnp.float32, smallest / len(split), high / len(split))
        gain = gain * jnp.repeat(jnp.exp(draws), shape[position] // blocks).reshape((-1,) + (1,) * (len(shape) - 1 - position))
    return gain


def gaussian(stream_key, dims, width, limit, shards=(), kind=jnp.bfloat16):
    drawn = jax.random.normal(stream_key, dims, jnp.float32) * width
    if len(shards) > 0:
        drawn = levels(stream_key, dims, shards, -0.22, 0.18) * drawn
    return jnp.clip(drawn, min=-limit, max=limit).astype(kind)


def setup_inputs(seed: int = 0) -> dict:
    splits = jax.random.split(jax.random.key(seed), 5)
    return {
        "samples": gaussian(splits[0], (A, NT), 1.0, 6.0, ((0, 64), (1, 8))),
        "tail": gaussian(splits[1], (A, (TAPS - 1) * L), 1.0, 6.0, ((0, 64),)),
        "taps": gaussian(splits[2], (TAPS, L), 0.5, 3.0, (), jnp.float32),
        "tile_table": draw_tile_table(jax.random.fold_in(splits[4], 71), 0),
    }


def dft_basis():
    sample_rows = jnp.arange(L, dtype=jnp.int32)[:, None]
    channel_cols = jnp.arange(F, dtype=jnp.int32)[None, :]
    angles = (sample_rows * channel_cols % L).astype(jnp.float32) * (2.0 * math.pi / L)
    norm_factor = 1.0 / math.sqrt(L)
    return jnp.concatenate([jnp.cos(angles) * norm_factor, -jnp.sin(angles) * norm_factor], axis=1).astype(jnp.bfloat16)

def correlate(own_block, partner):
    real_own = own_block[:, :, 0, :].astype(jnp.float32)
    imag_own = own_block[:, :, 1, :].astype(jnp.float32)
    real_far = partner[:, :, 0, :].astype(jnp.float32)
    imag_far = partner[:, :, 1, :].astype(jnp.float32)
    high = lax.Precision.HIGHEST
    real_part = jnp.einsum('isc,jsc->ijc', real_own, real_far, precision=high) + jnp.einsum('isc,jsc->ijc', imag_own, imag_far, precision=high)
    imag_part = jnp.einsum('isc,jsc->ijc', imag_own, real_far, precision=high) - jnp.einsum('isc,jsc->ijc', real_own, imag_far, precision=high)
    weight_mean = 1.0 / SPEC
    return jnp.stack([real_part * weight_mean, imag_part * weight_mean], axis=0)

def reference(samples, tail, taps, tile_table):
    basis = dft_basis().astype(jnp.float32)
    stream = jnp.concatenate([samples, tail], axis=1).reshape(NBLK, A_DEV, SPEC + TAPS - 1, L)

    def channelize(block_data):
        frame_data = block_data.astype(jnp.float32)
        filtered = taps[0][None, None, :] * frame_data[:, 0:SPEC, :]
        for tap in range(1, TAPS):
            filtered = filtered + taps[tap][None, None, :] * frame_data[:, tap:tap + SPEC, :]
        filtered = lax.optimization_barrier(filtered.astype(jnp.bfloat16)).astype(jnp.float32)
        spectra = jnp.dot(filtered.reshape(A_DEV * SPEC, L), basis, precision=lax.Precision.HIGHEST, preferred_element_type=jnp.float32)
        return spectra.astype(jnp.bfloat16).reshape(A_DEV, SPEC, 2, F)
    spectra = lax.map(channelize, stream)

    def device_tiles(block_index):
        own_block = lax.dynamic_index_in_dim(spectra, block_index, 0, keepdims=False)

        def single_tile(offset):
            partner_index = ((block_index + offset) % NBLK).astype(jnp.int32)
            partner = lax.dynamic_index_in_dim(spectra, partner_index, 0, keepdims=False)
            return correlate(own_block, partner)
        return lax.map(single_tile, lax.dynamic_index_in_dim(tile_table, block_index, 0, keepdims=False))
    return lax.map(device_tiles, jnp.arange(NBLK, dtype=jnp.int32))
```

```python
import functools
import math

import jax
import jax.numpy as jnp
import numpy as np
from jax import lax
from jax.experimental import pallas as pl
from jax.experimental.pallas import tpu as pltpu
from jax.sharding import PartitionSpec as P

F = 1024
L = 2048
TAPS = 4
A_DEV = 32
S_DEV = 4
SPAN = 4
PEERS = 8
C_DEV = F // PEERS
GROUP = 32
OWN = S_DEV * A_DEV
EARLY = (TAPS - 1) * A_DEV
ROWS = OWN + EARLY
K = 2 * PEERS * S_DEV
VMEM_LIMIT = 48 * 1024 * 1024


def dft_basis():
    sample_rows = np.arange(L, dtype=np.int64)[:, None]
    channel_cols = np.arange(F, dtype=np.int64)[None, :]
    phase_index = sample_rows * channel_cols % L
    table_angles = np.arange(L, dtype=np.float32) * np.float32(2.0 * math.pi / L)
    norm_factor = np.float32(1.0 / math.sqrt(L))
    cosine_table = np.cos(table_angles).astype(np.float32) * norm_factor
    sine_table = -np.sin(table_angles).astype(np.float32) * norm_factor
    cosines = cosine_table[phase_index].reshape(L, PEERS, C_DEV)
    sines = sine_table[phase_index].reshape(L, PEERS, C_DEV)
    whole_table = np.concatenate([cosines, sines], axis=2).transpose(1, 0, 2)
    return jnp.asarray(whole_table, dtype=jnp.bfloat16)


def channelize_kernel(place_ref, samples_ref, tail_ref, taps_ref, basis_ref, out_ref, filtered):
    def frame(ref, index):
        return ref[:, index * L : (index + 1) * L].astype(jnp.float32)

    def tap(index):
        return taps_ref[index : index + 1, :]

    def early_rows(ref):
        for row in range(TAPS - 1):
            total = tap(TAPS - 1) * frame(ref, row)
            for back in range(row):
                total = total + tap(TAPS - 1 - row + back) * frame(ref, back)
            start = OWN + row * A_DEV
            filtered[start : start + A_DEV, :] = total.astype(jnp.bfloat16)

    @pl.when(pl.program_id(0) == 0)
    def _():
        for row in range(S_DEV):
            total = tap(0) * frame(samples_ref, row)
            for ahead in range(1, S_DEV - row):
                total = total + tap(ahead) * frame(samples_ref, row + ahead)
            filtered[row * A_DEV : (row + 1) * A_DEV, :] = total.astype(jnp.bfloat16)

        @pl.when(place_ref[1] == 0)
        def _():
            early_rows(tail_ref)

        @pl.when(place_ref[1] != 0)
        def _():
            early_rows(samples_ref)

    spectra = jnp.dot(filtered[...], basis_ref[0], preferred_element_type=jnp.float32)
    spectra = spectra.astype(jnp.bfloat16)
    out_ref[0, 0] = spectra[:, :C_DEV]
    out_ref[0, 1] = spectra[:, C_DEV:]


def channelize(place, samples, tail, taps, basis):
    return pl.pallas_call(
        channelize_kernel,
        grid=(PEERS,),
        out_shape=jax.ShapeDtypeStruct((PEERS, 2, ROWS, C_DEV), jnp.bfloat16),
        in_specs=[
            pl.BlockSpec(memory_space=pltpu.SMEM),
            pl.BlockSpec((A_DEV, S_DEV * L), lambda i: (0, 0)),
            pl.BlockSpec((A_DEV, (TAPS - 1) * L), lambda i: (0, 0)),
            pl.BlockSpec((TAPS, L), lambda i: (0, 0)),
            pl.BlockSpec((1, L, 2 * C_DEV), lambda i: (i, 0, 0)),
        ],
        out_specs=pl.BlockSpec((1, 2, ROWS, C_DEV), lambda i: (i, 0, 0, 0)),
        scratch_shapes=[pltpu.VMEM((ROWS, L), jnp.bfloat16)],
        compiler_params=pltpu.CompilerParams(vmem_limit_bytes=VMEM_LIMIT),
        name="channelize",
    )(place, samples, tail, taps, basis)


def joined(x_ref, ri, t):
    own = x_ref[t, ri, 0:OWN, :].astype(jnp.float32)
    early = x_ref[(t + 1) % PEERS, ri, OWN:ROWS, :].astype(jnp.float32)
    return own[:A_DEV], own[A_DEV:] + early


def lane_groups(shape):
    return lax.broadcasted_iota(jnp.int32, shape, len(shape) - 1) // GROUP


def pack_kernel(place_ref, x_ref, w_ref, rows, turned):
    shift = place_ref[0]
    group = lane_groups((A_DEV, C_DEV))
    for ri in range(2):
        for t in range(PEERS):
            k = ri * PEERS + t
            first, rest = joined(x_ref, ri, t)
            by_row = [first] + [rest[j * A_DEV : (j + 1) * A_DEV] for j in range(S_DEV - 1)]
            rolled = [
                [by_row[j]] + [pltpu.roll(by_row[j], m * GROUP, 1) for m in range(1, SPAN)]
                for j in range(S_DEV)
            ]
            for c4 in range(SPAN):
                merged = rolled[0][(0 - c4) % SPAN]
                for j in range(1, S_DEV):
                    merged = jnp.where(group == j, rolled[j][(j - c4) % SPAN], merged)
                start = pl.multiple_of(lax.rem(shift + c4, SPAN) * A_DEV, A_DEV)
                rows[k, pl.ds(start, A_DEV), :] = merged
    for k in range(2 * PEERS):
        turned[k * C_DEV : (k + 1) * C_DEV, :] = rows[k].T

    def step(cq, carry):
        w_ref[cq] = turned[pl.ds(cq, K, stride=GROUP), :].astype(jnp.bfloat16)
        return carry

    lax.fori_loop(0, GROUP, step, 0, unroll=4)


def pack(place, received):
    return pl.pallas_call(
        pack_kernel,
        out_shape=jax.ShapeDtypeStruct((GROUP, K, SPAN * A_DEV), jnp.bfloat16),
        in_specs=[pl.BlockSpec(memory_space=pltpu.SMEM), pl.BlockSpec(memory_space=pltpu.VMEM)],
        out_specs=pl.BlockSpec(memory_space=pltpu.VMEM),
        scratch_shapes=[
            pltpu.VMEM((2 * PEERS, OWN, C_DEV), jnp.float32),
            pltpu.VMEM((2 * PEERS * OWN, C_DEV), jnp.float32),
        ],
        compiler_params=pltpu.CompilerParams(vmem_limit_bytes=VMEM_LIMIT),
        name="pack",
    )(place, received)


def left_kernel(x_ref, left_ref, rows, turned):
    scale = 1.0 / (PEERS * S_DEV)
    for ri in range(2):
        for t in range(PEERS):
            start = (ri * PEERS + t) * OWN
            first, rest = joined(x_ref, ri, t)
            rows[start : start + A_DEV, :] = first * scale
            rows[start + A_DEV : start + OWN, :] = rest * scale
    for a in range(A_DEV):
        real = rows[pl.ds(a, K, stride=A_DEV), :]
        imag = jnp.concatenate([real[K // 2 :], -real[: K // 2]], axis=0)
        turned[a * C_DEV : (a + 1) * C_DEV, :] = real.T
        turned[(A_DEV + a) * C_DEV : (A_DEV + a + 1) * C_DEV, :] = imag.T

    def step(c, carry):
        left_ref[c] = turned[pl.ds(c, 2 * A_DEV, stride=C_DEV), :].astype(jnp.bfloat16)
        return carry

    lax.fori_loop(0, C_DEV, step, 0, unroll=4)


def left_side(received):
    return pl.pallas_call(
        left_kernel,
        out_shape=jax.ShapeDtypeStruct((C_DEV, 2 * A_DEV, K), jnp.bfloat16),
        in_specs=[pl.BlockSpec(memory_space=pltpu.VMEM)],
        out_specs=pl.BlockSpec(memory_space=pltpu.VMEM),
        scratch_shapes=[
            pltpu.VMEM((2 * PEERS * OWN, C_DEV), jnp.float32),
            pltpu.VMEM((2 * A_DEV * C_DEV, K), jnp.float32),
        ],
        compiler_params=pltpu.CompilerParams(vmem_limit_bytes=VMEM_LIMIT),
        cost_estimate=pl.CostEstimate(flops=0, bytes_accessed=12 << 20, transcendentals=0),
        name="left_side",
    )(received)


I_STEP = 4


def correlate_kernel(place_ref, table_ref, left_ref, w0, w1, w2, w3, out_ref, slots, products):
    shift = place_ref[0]

    @pl.when(pl.program_id(0) == 0)
    def _():
        for e, ref in enumerate((w0, w1, w2, w3)):
            slots[lax.rem(shift + e, SPAN)] = ref[...]
        group = lane_groups((K, SPAN * A_DEV))

        def step(cq, carry):
            held = [slots[b, cq] for b in range(SPAN)]
            for c4 in range(SPAN):
                right = held[(0 - c4) % SPAN]
                for p in range(1, SPAN):
                    right = jnp.where(group == p, held[(p - c4) % SPAN], right)
                channel = c4 * GROUP + cq
                start = pl.multiple_of(channel * 2 * A_DEV, 2 * A_DEV)
                products[pl.ds(start, 2 * A_DEV), :] = jnp.dot(
                    left_ref[channel], right, preferred_element_type=jnp.float32
                )
            return carry

        lax.fori_loop(0, GROUP, step, 0, unroll=2)

    places = []
    for b in range(SPAN):
        offset = lax.rem(b - shift + SPAN, SPAN)
        position = jnp.int32(0)
        for tile in range(1, SPAN):
            position = position + jnp.where(table_ref[0, tile] == offset, tile, 0)
        places.append(position)
    group = lane_groups((A_DEV, C_DEV))
    base = pl.program_id(0) * I_STEP
    for part in range(2):
        for i in range(I_STEP):
            row = part * A_DEV + base + i
            turned = products[pl.ds(row, C_DEV, stride=2 * A_DEV), :].T
            pieces = [turned[p * A_DEV : (p + 1) * A_DEV] for p in range(SPAN)]
            for b in range(SPAN):
                tile = pieces[b]
                for c4 in range(1, SPAN):
                    tile = jnp.where(group == c4, pieces[(b + c4) % SPAN], tile)
                out_ref[0, places[b], part, i] = tile


def correlate(place, table, left, blocks):
    whole = pl.BlockSpec((GROUP, K, SPAN * A_DEV), lambda i: (0, 0, 0))
    return pl.pallas_call(
        correlate_kernel,
        grid=(A_DEV // I_STEP,),
        out_shape=jax.ShapeDtypeStruct((1, SPAN, 2, A_DEV, A_DEV, C_DEV), jnp.float32),
        in_specs=[
            pl.BlockSpec(memory_space=pltpu.SMEM),
            pl.BlockSpec(memory_space=pltpu.SMEM),
            pl.BlockSpec((C_DEV, 2 * A_DEV, K), lambda i: (0, 0, 0)),
        ]
        + [whole] * SPAN,
        out_specs=pl.BlockSpec(
            (1, SPAN, 2, I_STEP, A_DEV, C_DEV), lambda i: (0, 0, 0, i, 0, 0)
        ),
        scratch_shapes=[
            pltpu.VMEM((SPAN, GROUP, K, SPAN * A_DEV), jnp.bfloat16),
            pltpu.VMEM((C_DEV * 2 * A_DEV, SPAN * A_DEV), jnp.float32),
        ],
        compiler_params=pltpu.CompilerParams(vmem_limit_bytes=VMEM_LIMIT),
        name="correlate",
    )(place, table, left, *blocks)


def next_block(block):
    count = lax.axis_size("inp")
    return lax.ppermute(block, "inp", [((i + 1) % count, i) for i in range(count)])


def body(samples, tail, taps, tile_table):
    place = jnp.stack([lax.axis_index("inp") % SPAN, lax.axis_index("tm")]).astype(jnp.int32)
    partial = channelize(place, samples, tail, taps, dft_basis())
    received = lax.all_to_all(partial, "tm", split_axis=0, concat_axis=0, tiled=True)
    blocks = [pack(place, received)]
    left = left_side(received)
    for _ in range(1, SPAN):
        blocks.append(next_block(blocks[-1]))
    return correlate(place, tile_table, left, blocks)


def solution(mesh):
    in_specs = (P("inp", "tm"), P("inp", None), P(), P("inp", None))
    out_specs = P("inp", None, None, None, None, "tm")
    return jax.shard_map(body, mesh=mesh, in_specs=in_specs, out_specs=out_specs, check_vma=False)
```

```python
import functools
import math

import jax
import jax.numpy as jnp
import numpy as np
from jax import lax
from jax.experimental import pallas as pl
from jax.experimental.pallas import tpu as pltpu
from jax.sharding import PartitionSpec as P

F = 1024
L = 2048
TAPS = 4
A_DEV = 32
S_DEV = 4
SPAN = 4
PEERS = 8
C_DEV = F // PEERS
CHUNKS = PEERS // 2
GROUP = 32
HALF = 32
OWN = S_DEV * A_DEV
EARLY = (TAPS - 1) * A_DEV
ROWS = OWN + EARLY
K = 2 * PEERS * S_DEV
VMEM_LIMIT = 24 * 1024 * 1024
VMEM_WHOLE = 62 * 1024 * 1024


def dft_basis():
    half = L // 2
    sample_rows = np.arange(half, dtype=np.int64)[:, None]
    channel_cols = np.arange(F, dtype=np.int64)[None, :]
    phase_index = sample_rows * channel_cols % L
    table_angles = np.arange(L, dtype=np.float32) * np.float32(2.0 * math.pi / L)
    norm_factor = np.float32(1.0 / math.sqrt(L))
    cosine_table = np.cos(table_angles).astype(np.float32) * norm_factor
    sine_table = -np.sin(table_angles).astype(np.float32) * norm_factor
    split = (half, CHUNKS, 2, C_DEV // 2, 2)
    cosines = cosine_table[phase_index].reshape(split)
    sines = sine_table[phase_index].reshape(split)
    whole_table = np.stack([cosines, sines], axis=3).transpose(1, 5, 0, 2, 3, 4)
    return jnp.asarray(whole_table.reshape(CHUNKS, 2, half, 4 * (C_DEV // 2)), dtype=jnp.bfloat16)


def channelize_kernel(
    place_ref, samples_hbm, tail_hbm, taps_ref, basis_hbm, out_hbm,
    samples_ref, tail_ref, basis_ref, even_rows, odd_rows, out_ref, in_sems, basis_sems, out_sems,
):
    half = L // 2
    at_start = place_ref[1] == 0
    samples_copy = pltpu.make_async_copy(samples_hbm, samples_ref, in_sems.at[0])
    tail_copy = pltpu.make_async_copy(tail_hbm, tail_ref, in_sems.at[1])
    basis_copies = [
        pltpu.make_async_copy(basis_hbm.at[q], basis_ref.at[q], basis_sems.at[q])
        for q in range(CHUNKS)
    ]
    samples_copy.start()

    @pl.when(at_start)
    def _():
        tail_copy.start()

    for copy in basis_copies:
        copy.start()

    def frame(ref, index):
        return ref[:, index * L : (index + 1) * L].astype(jnp.float32)

    def tap(index):
        return taps_ref[index : index + 1, :]

    def fold(start, total):
        low, high = total[:, :half], total[:, half:]
        even_rows[start : start + A_DEV, :] = (low + high).astype(jnp.bfloat16)
        odd_rows[start : start + A_DEV, :] = (low - high).astype(jnp.bfloat16)

    def early_rows(ref):
        for row in range(TAPS - 1):
            total = tap(TAPS - 1) * frame(ref, row)
            for back in range(row):
                total = total + tap(TAPS - 1 - row + back) * frame(ref, back)
            fold(OWN + row * A_DEV, total)

    samples_copy.wait()
    for row in range(S_DEV):
        total = tap(0) * frame(samples_ref, row)
        for ahead in range(1, S_DEV - row):
            total = total + tap(ahead) * frame(samples_ref, row + ahead)
        fold(row * A_DEV, total)

    @pl.when(at_start)
    def _():
        tail_copy.wait()
        early_rows(tail_ref)

    @pl.when(jnp.logical_not(at_start))
    def _():
        early_rows(samples_ref)

    out_copies = []
    low_lanes = lax.broadcasted_iota(jnp.int32, (ROWS, C_DEV), 1) < C_DEV // 2
    for q in range(CHUNKS):
        basis_copies[q].wait()
        even = jnp.dot(even_rows[...], basis_ref[q, 0], preferred_element_type=jnp.float32)
        odd = jnp.dot(odd_rows[...], basis_ref[q, 1], preferred_element_type=jnp.float32)
        for h in range(2):
            e = even[:, h * C_DEV : (h + 1) * C_DEV]
            o = odd[:, h * C_DEV : (h + 1) * C_DEV]
            real = jnp.where(low_lanes, e, pltpu.roll(o, C_DEV // 2, 1))
            imag = jnp.where(low_lanes, pltpu.roll(e, C_DEV // 2, 1), o)
            out_ref[2 * q + h, 0] = real.astype(jnp.bfloat16)
            out_ref[2 * q + h, 1] = imag.astype(jnp.bfloat16)
        copy = pltpu.make_async_copy(
            out_ref.at[pl.ds(2 * q, 2)], out_hbm.at[pl.ds(2 * q, 2)], out_sems.at[q]
        )
        copy.start()
        out_copies.append(copy)
    for copy in out_copies:
        copy.wait()


def channelize(place, samples, tail, taps, basis):
    anywhere = pl.BlockSpec(memory_space=pltpu.HBM)
    out = (PEERS, 2, ROWS, C_DEV)
    return pl.pallas_call(
        channelize_kernel,
        out_shape=jax.ShapeDtypeStruct(out, jnp.bfloat16),
        in_specs=[
            pl.BlockSpec(memory_space=pltpu.SMEM),
            anywhere,
            anywhere,
            pl.BlockSpec(memory_space=pltpu.VMEM),
            anywhere,
        ],
        out_specs=anywhere,
        scratch_shapes=[
            pltpu.VMEM(samples.shape, jnp.bfloat16),
            pltpu.VMEM(tail.shape, jnp.bfloat16),
            pltpu.VMEM(basis.shape, jnp.bfloat16),
            pltpu.VMEM((ROWS, L // 2), jnp.bfloat16),
            pltpu.VMEM((ROWS, L // 2), jnp.bfloat16),
            pltpu.VMEM(out, jnp.bfloat16),
            pltpu.SemaphoreType.DMA((2,)),
            pltpu.SemaphoreType.DMA((CHUNKS,)),
            pltpu.SemaphoreType.DMA((CHUNKS,)),
        ],
        compiler_params=pltpu.CompilerParams(vmem_limit_bytes=VMEM_WHOLE),
        name="channelize",
    )(place, samples, tail, taps, basis)


def joined(x_ref, ri, t):
    own = x_ref[t, ri, 0:OWN, :].astype(jnp.float32)
    early = x_ref[(t + 1) % PEERS, ri, OWN:ROWS, :].astype(jnp.float32)
    return own[:A_DEV], own[A_DEV:] + early


def lane_groups(shape):
    return lax.broadcasted_iota(jnp.int32, shape, len(shape) - 1) // GROUP


def pack_kernel(place_ref, x_ref, w_ref, rows, turned):
    shift = place_ref[0]
    group = lane_groups((A_DEV, C_DEV))
    for ri in range(2):
        for t in range(PEERS):
            k = ri * PEERS + t
            first, rest = joined(x_ref, ri, t)
            by_row = [first] + [rest[j * A_DEV : (j + 1) * A_DEV] for j in range(S_DEV - 1)]
            rolled = [
                [by_row[j]] + [pltpu.roll(by_row[j], m * GROUP, 1) for m in range(1, SPAN)]
                for j in range(S_DEV)
            ]
            for c4 in range(SPAN):
                merged = rolled[0][(0 - c4) % SPAN]
                for j in range(1, S_DEV):
                    merged = jnp.where(group == j, rolled[j][(j - c4) % SPAN], merged)
                start = pl.multiple_of(lax.rem(shift + c4, SPAN) * A_DEV, A_DEV)
                rows[k, pl.ds(start, A_DEV), :] = merged
    for k in range(2 * PEERS):
        turned[k * C_DEV : (k + 1) * C_DEV, :] = rows[k].T

    def step(cq, carry):
        w_ref[cq] = turned[pl.ds(cq, K, stride=GROUP), :].astype(jnp.bfloat16)
        return carry

    lax.fori_loop(0, GROUP, step, 0, unroll=4)


def pack(place, received):
    return pl.pallas_call(
        pack_kernel,
        out_shape=jax.ShapeDtypeStruct((GROUP, K, SPAN * A_DEV), jnp.bfloat16),
        in_specs=[pl.BlockSpec(memory_space=pltpu.SMEM), pl.BlockSpec(memory_space=pltpu.VMEM)],
        out_specs=pl.BlockSpec(memory_space=pltpu.VMEM),
        scratch_shapes=[
            pltpu.VMEM((2 * PEERS, OWN, C_DEV), jnp.float32),
            pltpu.VMEM((2 * PEERS * OWN, C_DEV), jnp.float32),
        ],
        compiler_params=pltpu.CompilerParams(vmem_limit_bytes=VMEM_LIMIT),
        name="pack",
    )(place, received)


def left_kernel(x_ref, left_ref, rows, turned):
    scale = 1.0 / (PEERS * S_DEV)
    for ri in range(2):
        for t in range(PEERS):
            start = (ri * PEERS + t) * OWN
            first, rest = joined(x_ref, ri, t)
            rows[start : start + A_DEV, :] = first * scale
            rows[start + A_DEV : start + OWN, :] = rest * scale
    for a in range(A_DEV):
        real = rows[pl.ds(a, K, stride=A_DEV), :]
        turned[a * C_DEV : (a + 1) * C_DEV, :] = real.T

    def step(c, carry):
        left_ref[c] = turned[pl.ds(c, A_DEV, stride=C_DEV), :].astype(jnp.bfloat16)
        return carry

    lax.fori_loop(0, C_DEV, step, 0, unroll=4)


def left_side(received):
    return pl.pallas_call(
        left_kernel,
        out_shape=jax.ShapeDtypeStruct((C_DEV, A_DEV, K), jnp.bfloat16),
        in_specs=[pl.BlockSpec(memory_space=pltpu.VMEM)],
        out_specs=pl.BlockSpec(memory_space=pltpu.VMEM),
        scratch_shapes=[
            pltpu.VMEM((2 * PEERS * OWN, C_DEV), jnp.float32),
            pltpu.VMEM((A_DEV * C_DEV, K), jnp.float32),
        ],
        compiler_params=pltpu.CompilerParams(vmem_limit_bytes=VMEM_LIMIT),
        cost_estimate=pl.CostEstimate(flops=0, bytes_accessed=64 << 20, transcendentals=0),
        name="left_side",
    )(received)


I_STEP = 4


def correlate_kernel(
    place_ref, table_ref, left_ref, own, core, cross, cross_w, swap, swap_w, far, far_d,
    out_ref, slots, products, sems,
):
    shift = place_ref[0]

    @pl.when(pl.program_id(0) == 0)
    def _():
        where = place_ref[2]
        late = where >= HALF - 2
        odd = lax.rem(where, 2) == 1
        direct = odd & (where >= HALF - 3)

        def bring(e, condition, source):
            @pl.when(condition)
            def _():
                pltpu.make_async_copy(
                    source, slots.at[lax.rem(shift + e, SPAN)], sems.at[e]
                ).start()

        both, neither = jnp.logical_and, jnp.logical_not
        bring(0, where >= 0, own)
        bring(1, neither(odd), core)
        bring(1, both(odd, neither(late)), cross)
        bring(1, both(odd, late), cross_w)
        bring(2, neither(late), swap)
        bring(2, late, swap_w)
        bring(3, both(neither(odd), neither(late)), cross)
        bring(3, both(neither(odd), late), cross_w)
        bring(3, both(odd, neither(direct)), far)
        bring(3, direct, far_d)
        for e in range(SPAN):
            pltpu.make_async_copy(own, slots.at[lax.rem(shift + e, SPAN)], sems.at[e]).wait()
        group = lane_groups((K, SPAN * A_DEV))

        def step(cq, carry):
            held = [slots[b, cq] for b in range(SPAN)]
            for c4 in range(SPAN):
                right = held[(0 - c4) % SPAN]
                for p in range(1, SPAN):
                    right = jnp.where(group == p, held[(p - c4) % SPAN], right)
                lane = c4 * GROUP + cq
                channel = 2 * lax.rem(lane, C_DEV // 2) + c4 // 2
                crossed = jnp.concatenate([-right[K // 2 :], right[: K // 2]], axis=0)
                start = pl.multiple_of(channel * A_DEV, A_DEV)
                product = jnp.dot(
                    left_ref[lane],
                    jnp.concatenate([right, crossed], axis=1),
                    preferred_element_type=jnp.float32,
                )
                products[pl.ds(start, A_DEV), :] = product[:, : SPAN * A_DEV]
                products[pl.ds(C_DEV * A_DEV + start, A_DEV), :] = product[:, SPAN * A_DEV :]
            return carry

        lax.fori_loop(0, GROUP, step, 0, unroll=2)

    places = []
    for b in range(SPAN):
        offset = lax.rem(b - shift + SPAN, SPAN)
        position = jnp.int32(0)
        for tile in range(1, SPAN):
            position = position + jnp.where(table_ref[0, tile] == offset, tile, 0)
        places.append(position)
    channel = lax.broadcasted_iota(jnp.int32, (A_DEV, C_DEV), 1)
    group = 2 * (channel % 2) + channel // (C_DEV // 2)
    base = pl.program_id(0) * I_STEP
    for part in range(2):
        for i in range(I_STEP):
            row = part * C_DEV * A_DEV + base + i
            turned = products[pl.ds(row, C_DEV, stride=A_DEV), :].T
            pieces = [turned[p * A_DEV : (p + 1) * A_DEV] for p in range(SPAN)]
            for b in range(SPAN):
                tile = pieces[b]
                for c4 in range(1, SPAN):
                    tile = jnp.where(group == c4, pieces[(b + c4) % SPAN], tile)
                out_ref[0, places[b], part, i] = tile


def correlate(place, table, left, blocks):
    return pl.pallas_call(
        correlate_kernel,
        grid=(A_DEV // I_STEP,),
        out_shape=jax.ShapeDtypeStruct((1, SPAN, 2, A_DEV, A_DEV, C_DEV), jnp.float32),
        in_specs=[
            pl.BlockSpec(memory_space=pltpu.SMEM),
            pl.BlockSpec(memory_space=pltpu.SMEM),
            pl.BlockSpec(memory_space=pltpu.VMEM),
        ]
        + [pl.BlockSpec(memory_space=pltpu.HBM)] * len(blocks),
        out_specs=pl.BlockSpec(
            (1, SPAN, 2, I_STEP, A_DEV, C_DEV), lambda i: (0, 0, 0, i, 0, 0)
        ),
        scratch_shapes=[
            pltpu.VMEM((SPAN, GROUP, K, SPAN * A_DEV), jnp.bfloat16),
            pltpu.VMEM((2 * C_DEV * A_DEV, SPAN * A_DEV), jnp.float32),
            pltpu.SemaphoreType.DMA((SPAN,)),
        ],
        compiler_params=pltpu.CompilerParams(vmem_limit_bytes=VMEM_LIMIT),
        name="correlate",
    )(place, table, left, *blocks)


def send(block, pairs):
    return lax.ppermute(block, "inp", pairs)


def late(d):
    return d % HALF >= HALF - 2


def partners(own, received):
    count = lax.axis_size("inp")
    every = range(count)
    over = [((d + (1 if d % 2 else 3)) % count, d) for d in every]
    cross = send(own, [(s, d) for s, d in over if not late(d)])
    core = send(own, [(d + 1, d) for d in every if d % 2 == 0])
    cross_w = send(own, [(s, d) for s, d in over if late(d)])
    three = [((d + 3) % count, d) for d in every if d % 2]
    far_d = send(own, [(s, d) for s, d in three if d % HALF >= HALF - 3])
    received, _ = lax.optimization_barrier((received, own))
    cross, left = lax.optimization_barrier((cross, left_side(received)))
    far = send(cross, [(d + 2, d) for d in every if d % 2 and d % HALF < HALF - 3])
    swap = send(cross, [(d ^ 1, d) for d in every if not late(d)])
    passed_w, swap, far_d, core = lax.optimization_barrier((cross_w, swap, far_d, core))
    swap_w = send(passed_w, [(d ^ 1, d) for d in every if late(d)])
    return left, [own, core, cross, passed_w, swap, swap_w, far, far_d]


def body(samples, tail, taps, tile_table):
    block = lax.axis_index("inp")
    place = jnp.stack([block % SPAN, lax.axis_index("tm"), block % HALF]).astype(jnp.int32)
    partial = channelize(place, samples, tail, taps, dft_basis())
    received = lax.all_to_all(partial, "tm", split_axis=0, concat_axis=0, tiled=True)
    own = pack(place, received)
    left, blocks = partners(own, received)
    return correlate(place, tile_table, left, blocks)


def solution(mesh):
    in_specs = (P("inp", "tm"), P("inp", None), P(), P("inp", None))
    out_specs = P("inp", None, None, None, None, "tm")
    return jax.shard_map(body, mesh=mesh, in_specs=in_specs, out_specs=out_specs, check_vma=False)
```

```python
import functools
import math

import jax
import jax.numpy as jnp
import numpy as np
from jax import lax
from jax.experimental import pallas as pl
from jax.experimental.pallas import tpu as pltpu
from jax.sharding import PartitionSpec as P

F = 1024
L = 2048
TAPS = 4
A_DEV = 32
S_DEV = 4
SPAN = 4
PEERS = 8
C_DEV = F // PEERS
CHUNKS = PEERS // 2
GROUP = 32
HALF = 32
OWN = S_DEV * A_DEV
EARLY = (TAPS - 1) * A_DEV
ROWS = OWN + EARLY
K = 2 * PEERS * S_DEV
VMEM_LIMIT = 24 * 1024 * 1024
VMEM_WHOLE = 62 * 1024 * 1024


def dft_basis():
    half = L // 2
    sample_rows = np.arange(half, dtype=np.int64)[:, None]
    channel_cols = np.arange(F, dtype=np.int64)[None, :]
    phase_index = sample_rows * channel_cols % L
    table_angles = np.arange(L, dtype=np.float32) * np.float32(2.0 * math.pi / L)
    norm_factor = np.float32(1.0 / math.sqrt(L))
    cosine_table = np.cos(table_angles).astype(np.float32) * norm_factor
    sine_table = -np.sin(table_angles).astype(np.float32) * norm_factor
    split = (half, CHUNKS, 2, C_DEV // 2, 2)
    cosines = cosine_table[phase_index].reshape(split)
    sines = sine_table[phase_index].reshape(split)
    whole_table = np.stack([cosines, sines], axis=3).transpose(1, 5, 0, 2, 3, 4)
    return jnp.asarray(whole_table.reshape(CHUNKS, 2, half, 4 * (C_DEV // 2)), dtype=jnp.bfloat16)


def channelize_kernel(
    place_ref, samples_hbm, tail_hbm, taps_ref, basis_hbm, out_hbm,
    samples_ref, tail_ref, basis_ref, even_rows, odd_rows, out_ref, in_sems, basis_sems, out_sems,
):
    half = L // 2
    at_start = place_ref[1] == 0
    samples_copy = pltpu.make_async_copy(samples_hbm, samples_ref, in_sems.at[0])
    tail_copy = pltpu.make_async_copy(tail_hbm, tail_ref, in_sems.at[1])
    basis_copies = [
        pltpu.make_async_copy(basis_hbm.at[q], basis_ref.at[q], basis_sems.at[q])
        for q in range(CHUNKS)
    ]
    samples_copy.start()

    @pl.when(at_start)
    def _():
        tail_copy.start()

    for copy in basis_copies:
        copy.start()

    def frame(ref, index):
        return ref[:, index * L : (index + 1) * L].astype(jnp.float32)

    def tap(index):
        return taps_ref[index : index + 1, :]

    def fold(start, total):
        low, high = total[:, :half], total[:, half:]
        even_rows[start : start + A_DEV, :] = (low + high).astype(jnp.bfloat16)
        odd_rows[start : start + A_DEV, :] = (low - high).astype(jnp.bfloat16)

    def early_rows(ref):
        for row in range(TAPS - 1):
            total = tap(TAPS - 1) * frame(ref, row)
            for back in range(row):
                total = total + tap(TAPS - 1 - row + back) * frame(ref, back)
            fold(OWN + row * A_DEV, total)

    samples_copy.wait()
    for row in range(S_DEV):
        total = tap(0) * frame(samples_ref, row)
        for ahead in range(1, S_DEV - row):
            total = total + tap(ahead) * frame(samples_ref, row + ahead)
        fold(row * A_DEV, total)

    @pl.when(at_start)
    def _():
        tail_copy.wait()
        early_rows(tail_ref)

    @pl.when(jnp.logical_not(at_start))
    def _():
        early_rows(samples_ref)

    out_copies = []
    low_lanes = lax.broadcasted_iota(jnp.int32, (ROWS, C_DEV), 1) < C_DEV // 2
    for q in range(CHUNKS):
        basis_copies[q].wait()
        even = jnp.dot(even_rows[...], basis_ref[q, 0], preferred_element_type=jnp.float32)
        odd = jnp.dot(odd_rows[...], basis_ref[q, 1], preferred_element_type=jnp.float32)
        for h in range(2):
            e = even[:, h * C_DEV : (h + 1) * C_DEV]
            o = odd[:, h * C_DEV : (h + 1) * C_DEV]
            real = jnp.where(low_lanes, e, pltpu.roll(o, C_DEV // 2, 1))
            imag = jnp.where(low_lanes, pltpu.roll(e, C_DEV // 2, 1), o)
            out_ref[2 * q + h, 0] = real.astype(jnp.bfloat16)
            out_ref[2 * q + h, 1] = imag.astype(jnp.bfloat16)
        copy = pltpu.make_async_copy(
            out_ref.at[pl.ds(2 * q, 2)], out_hbm.at[pl.ds(2 * q, 2)], out_sems.at[q]
        )
        copy.start()
        out_copies.append(copy)
    for copy in out_copies:
        copy.wait()


def channelize(place, samples, tail, taps, basis):
    anywhere = pl.BlockSpec(memory_space=pltpu.HBM)
    out = (PEERS, 2, ROWS, C_DEV)
    return pl.pallas_call(
        channelize_kernel,
        out_shape=jax.ShapeDtypeStruct(out, jnp.bfloat16),
        in_specs=[
            pl.BlockSpec(memory_space=pltpu.SMEM),
            anywhere,
            anywhere,
            pl.BlockSpec(memory_space=pltpu.VMEM),
            anywhere,
        ],
        out_specs=anywhere,
        scratch_shapes=[
            pltpu.VMEM(samples.shape, jnp.bfloat16),
            pltpu.VMEM(tail.shape, jnp.bfloat16),
            pltpu.VMEM(basis.shape, jnp.bfloat16),
            pltpu.VMEM((ROWS, L // 2), jnp.bfloat16),
            pltpu.VMEM((ROWS, L // 2), jnp.bfloat16),
            pltpu.VMEM(out, jnp.bfloat16),
            pltpu.SemaphoreType.DMA((2,)),
            pltpu.SemaphoreType.DMA((CHUNKS,)),
            pltpu.SemaphoreType.DMA((CHUNKS,)),
        ],
        compiler_params=pltpu.CompilerParams(vmem_limit_bytes=VMEM_WHOLE),
        name="channelize",
    )(place, samples, tail, taps, basis)


def joined(x_ref, ri, t):
    own = x_ref[t, ri, 0:OWN, :].astype(jnp.float32)
    early = x_ref[(t + 1) % PEERS, ri, OWN:ROWS, :].astype(jnp.float32)
    return own[:A_DEV], own[A_DEV:] + early


def lane_groups(shape):
    return lax.broadcasted_iota(jnp.int32, shape, len(shape) - 1) // GROUP


def pack_kernel(place_ref, x_ref, w_ref, rows, turned):
    shift = place_ref[0]
    group = lane_groups((A_DEV, C_DEV))
    for ri in range(2):
        for t in range(PEERS):
            k = ri * PEERS + t
            first, rest = joined(x_ref, ri, t)
            by_row = [first] + [rest[j * A_DEV : (j + 1) * A_DEV] for j in range(S_DEV - 1)]
            rolled = [
                [by_row[j]] + [pltpu.roll(by_row[j], m * GROUP, 1) for m in range(1, SPAN)]
                for j in range(S_DEV)
            ]
            for c4 in range(SPAN):
                merged = rolled[0][(0 - c4) % SPAN]
                for j in range(1, S_DEV):
                    merged = jnp.where(group == j, rolled[j][(j - c4) % SPAN], merged)
                start = pl.multiple_of(lax.rem(shift + c4, SPAN) * A_DEV, A_DEV)
                rows[k, pl.ds(start, A_DEV), :] = merged
    for k in range(2 * PEERS):
        turned[k * C_DEV : (k + 1) * C_DEV, :] = rows[k].T

    def step(cq, carry):
        w_ref[cq] = turned[pl.ds(cq, K, stride=GROUP), :].astype(jnp.bfloat16)
        return carry

    lax.fori_loop(0, GROUP, step, 0, unroll=8)


def pack(place, received):
    return pl.pallas_call(
        pack_kernel,
        out_shape=jax.ShapeDtypeStruct((GROUP, K, SPAN * A_DEV), jnp.bfloat16),
        in_specs=[pl.BlockSpec(memory_space=pltpu.SMEM), pl.BlockSpec(memory_space=pltpu.VMEM)],
        out_specs=pl.BlockSpec(memory_space=pltpu.VMEM),
        scratch_shapes=[
            pltpu.VMEM((2 * PEERS, OWN, C_DEV), jnp.float32),
            pltpu.VMEM((2 * PEERS * OWN, C_DEV), jnp.float32),
        ],
        compiler_params=pltpu.CompilerParams(vmem_limit_bytes=VMEM_LIMIT),
        name="pack",
    )(place, received)


def left_kernel(x_ref, left_ref, rows, turned):
    scale = 1.0 / (PEERS * S_DEV)
    for ri in range(2):
        for t in range(PEERS):
            start = (ri * PEERS + t) * OWN
            first, rest = joined(x_ref, ri, t)
            rows[start : start + A_DEV, :] = first * scale
            rows[start + A_DEV : start + OWN, :] = rest * scale
    for a in range(A_DEV):
        real = rows[pl.ds(a, K, stride=A_DEV), :]
        turned[a * C_DEV : (a + 1) * C_DEV, :] = real.T

    def step(c, carry):
        left_ref[c] = turned[pl.ds(c, A_DEV, stride=C_DEV), :].astype(jnp.bfloat16)
        return carry

    lax.fori_loop(0, C_DEV, step, 0, unroll=8)


def left_side(received):
    return pl.pallas_call(
        left_kernel,
        out_shape=jax.ShapeDtypeStruct((C_DEV, A_DEV, K), jnp.bfloat16),
        in_specs=[pl.BlockSpec(memory_space=pltpu.VMEM)],
        out_specs=pl.BlockSpec(memory_space=pltpu.VMEM),
        scratch_shapes=[
            pltpu.VMEM((2 * PEERS * OWN, C_DEV), jnp.float32),
            pltpu.VMEM((A_DEV * C_DEV, K), jnp.float32),
        ],
        compiler_params=pltpu.CompilerParams(vmem_limit_bytes=VMEM_LIMIT),
        cost_estimate=pl.CostEstimate(flops=0, bytes_accessed=64 << 20, transcendentals=0),
        name="left_side",
    )(received)


I_STEP = 8


def correlate_kernel(
    place_ref, table_ref, left_ref, own, core, cross, cross_w, swap, swap_w, far, far_w,
    out_ref, slots, products, sems,
):
    shift = place_ref[0]

    @pl.when(pl.program_id(0) == 0)
    def _():
        where = place_ref[2]
        late = where >= HALF - 2
        odd = lax.rem(where, 2) == 1
        before = where == HALF - 3

        def bring(e, condition, source):
            @pl.when(condition)
            def _():
                pltpu.make_async_copy(
                    source, slots.at[lax.rem(shift + e, SPAN)], sems.at[e]
                ).start()

        both, neither = jnp.logical_and, jnp.logical_not
        bring(0, where >= 0, own)
        bring(1, neither(odd), core)
        bring(1, both(odd, neither(late)), cross)
        bring(1, both(odd, late), cross_w)
        bring(2, neither(late), swap)
        bring(2, late, swap_w)
        bring(3, both(neither(odd), neither(late)), cross)
        bring(3, both(neither(odd), late), cross_w)
        bring(3, both(odd, neither(late | before)), far)
        bring(3, before, far_w)
        bring(3, both(odd, late), core)
        for e in range(SPAN):
            pltpu.make_async_copy(own, slots.at[lax.rem(shift + e, SPAN)], sems.at[e]).wait()
        group = lane_groups((K, SPAN * A_DEV))

        def step(cq, carry):
            held = [slots[b, cq] for b in range(SPAN)]
            for c4 in range(SPAN):
                right = held[(0 - c4) % SPAN]
                for p in range(1, SPAN):
                    right = jnp.where(group == p, held[(p - c4) % SPAN], right)
                lane = c4 * GROUP + cq
                channel = 2 * lax.rem(lane, C_DEV // 2) + c4 // 2
                crossed = jnp.concatenate([-right[K // 2 :], right[: K // 2]], axis=0)
                start = pl.multiple_of(channel * A_DEV, A_DEV)
                product = jnp.dot(
                    left_ref[lane],
                    jnp.concatenate([right, crossed], axis=1),
                    preferred_element_type=jnp.float32,
                )
                products[pl.ds(start, A_DEV), :] = product[:, : SPAN * A_DEV]
                products[pl.ds(C_DEV * A_DEV + start, A_DEV), :] = product[:, SPAN * A_DEV :]
            return carry

        lax.fori_loop(0, GROUP, step, 0, unroll=8)

    places = []
    for b in range(SPAN):
        offset = lax.rem(b - shift + SPAN, SPAN)
        position = jnp.int32(0)
        for tile in range(1, SPAN):
            position = position + jnp.where(table_ref[0, tile] == offset, tile, 0)
        places.append(position)
    channel = lax.broadcasted_iota(jnp.int32, (A_DEV, C_DEV), 1)
    group = 2 * (channel % 2) + channel // (C_DEV // 2)
    base = pl.program_id(0) * I_STEP
    for part in range(2):
        for i in range(I_STEP):
            row = part * C_DEV * A_DEV + base + i
            turned = products[pl.ds(row, C_DEV, stride=A_DEV), :].T
            pieces = [turned[p * A_DEV : (p + 1) * A_DEV] for p in range(SPAN)]
            for b in range(SPAN):
                tile = pieces[b]
                for c4 in range(1, SPAN):
                    tile = jnp.where(group == c4, pieces[(b + c4) % SPAN], tile)
                out_ref[0, places[b], part, i] = tile


def correlate(place, table, left, blocks):
    return pl.pallas_call(
        correlate_kernel,
        grid=(A_DEV // I_STEP,),
        out_shape=jax.ShapeDtypeStruct((1, SPAN, 2, A_DEV, A_DEV, C_DEV), jnp.float32),
        in_specs=[
            pl.BlockSpec(memory_space=pltpu.SMEM),
            pl.BlockSpec(memory_space=pltpu.SMEM),
            pl.BlockSpec(memory_space=pltpu.VMEM),
        ]
        + [pl.BlockSpec(memory_space=pltpu.HBM)] * len(blocks),
        out_specs=pl.BlockSpec(
            (1, SPAN, 2, I_STEP, A_DEV, C_DEV), lambda i: (0, 0, 0, i, 0, 0)
        ),
        scratch_shapes=[
            pltpu.VMEM((SPAN, GROUP, K, SPAN * A_DEV), jnp.bfloat16),
            pltpu.VMEM((2 * C_DEV * A_DEV, SPAN * A_DEV), jnp.float32),
            pltpu.SemaphoreType.DMA((SPAN,)),
        ],
        compiler_params=pltpu.CompilerParams(vmem_limit_bytes=VMEM_LIMIT),
        name="correlate",
    )(place, table, left, *blocks)


def send(block, pairs):
    return lax.ppermute(block, "inp", pairs)


def late(d):
    return d % HALF >= HALF - 2


def partners(own, received):
    count = lax.axis_size("inp")
    every = range(count)
    over = [((d + (1 if d % 2 else 3)) % count, d) for d in every]
    cross = send(own, [(s, d) for s, d in over if not late(d)])
    third = [((d + 3) % count, d) for d in every if d % 2 and late(d)]
    core = send(own, [(d + 1, d) for d in every if d % 2 == 0] + third)
    cross_w = send(own, [(s, d) for s, d in over if late(d)])
    received, _ = lax.optimization_barrier((received, own))
    cross, left = lax.optimization_barrier((cross, left_side(received)))
    ahead = [(d + 2, d) for d in every if d % 2 and not late(d)]
    far = send(cross, [(s, d) for s, d in ahead if not late(s)])
    swap = send(cross, [(d ^ 1, d) for d in every if not late(d)])
    far_w = send(cross_w, [(s, d) for s, d in ahead if late(s)])
    passed_w, core, far = lax.optimization_barrier((cross_w, core, far))
    swap_w = send(passed_w, [(d ^ 1, d) for d in every if late(d)])
    return left, [own, core, cross, passed_w, swap, swap_w, far, far_w]


def body(samples, tail, taps, tile_table):
    block = lax.axis_index("inp")
    place = jnp.stack([block % SPAN, lax.axis_index("tm"), block % HALF]).astype(jnp.int32)
    partial = channelize(place, samples, tail, taps, dft_basis())
    received = lax.all_to_all(partial, "tm", split_axis=0, concat_axis=0, tiled=True)
    own = pack(place, received)
    left, blocks = partners(own, received)
    return correlate(place, tile_table, left, blocks)


def solution(mesh):
    in_specs = (P("inp", "tm"), P("inp", None), P(), P("inp", None))
    out_specs = P("inp", None, None, None, None, "tm")
    return jax.shard_map(body, mesh=mesh, in_specs=in_specs, out_specs=out_specs, check_vma=False)
```

```python
import functools
import math

import jax
import jax.numpy as jnp
import numpy as np
from jax import lax
from jax.experimental import pallas as pl
from jax.experimental.pallas import tpu as pltpu
from jax.sharding import PartitionSpec as P

F = 1024
L = 2048
TAPS = 4
A_DEV = 32
S_DEV = 4
SPAN = 4
PEERS = 8
C_DEV = F // PEERS
CHUNKS = PEERS // 2
GROUP = 32
HALF = 32
OWN = S_DEV * A_DEV
EARLY = (TAPS - 1) * A_DEV
ROWS = OWN + EARLY
K = 2 * PEERS * S_DEV
VMEM_LIMIT = 24 * 1024 * 1024
VMEM_WHOLE = 62 * 1024 * 1024


def dft_basis():
    half = L // 2
    sample_rows = np.arange(half, dtype=np.int64)[:, None]
    channel_cols = np.arange(F, dtype=np.int64)[None, :]
    phase_index = sample_rows * channel_cols % L
    table_angles = np.arange(L, dtype=np.float32) * np.float32(2.0 * math.pi / L)
    norm_factor = np.float32(1.0 / math.sqrt(L))
    cosine_table = np.cos(table_angles).astype(np.float32) * norm_factor
    sine_table = -np.sin(table_angles).astype(np.float32) * norm_factor
    split = (half, CHUNKS, 2, C_DEV // 2, 2)
    cosines = cosine_table[phase_index].reshape(split)
    sines = sine_table[phase_index].reshape(split)
    whole_table = np.stack([cosines, sines], axis=3).transpose(1, 5, 0, 2, 3, 4)
    return jnp.asarray(whole_table.reshape(CHUNKS, 2, half, 4 * (C_DEV // 2)), dtype=jnp.bfloat16)


def channelize_kernel(
    place_ref, samples_hbm, tail_hbm, taps_ref, basis_hbm, out_hbm,
    samples_ref, tail_ref, basis_ref, even_rows, odd_rows, out_ref, in_sems, basis_sems, out_sems,
):
    half = L // 2
    at_start = place_ref[1] == 0
    samples_copy = pltpu.make_async_copy(samples_hbm, samples_ref, in_sems.at[0])
    tail_copy = pltpu.make_async_copy(tail_hbm, tail_ref, in_sems.at[1])
    basis_copies = [
        pltpu.make_async_copy(basis_hbm.at[q], basis_ref.at[q], basis_sems.at[q])
        for q in range(CHUNKS)
    ]
    samples_copy.start()

    @pl.when(at_start)
    def _():
        tail_copy.start()

    for copy in basis_copies:
        copy.start()

    def frame(ref, index):
        return ref[:, index * L : (index + 1) * L].astype(jnp.float32)

    def tap(index):
        return taps_ref[index : index + 1, :]

    def fold(start, total):
        low, high = total[:, :half], total[:, half:]
        even_rows[start : start + A_DEV, :] = (low + high).astype(jnp.bfloat16)
        odd_rows[start : start + A_DEV, :] = (low - high).astype(jnp.bfloat16)

    def early_rows(ref):
        for row in range(TAPS - 1):
            total = tap(TAPS - 1) * frame(ref, row)
            for back in range(row):
                total = total + tap(TAPS - 1 - row + back) * frame(ref, back)
            fold(OWN + row * A_DEV, total)

    samples_copy.wait()
    for row in range(S_DEV):
        total = tap(0) * frame(samples_ref, row)
        for ahead in range(1, S_DEV - row):
            total = total + tap(ahead) * frame(samples_ref, row + ahead)
        fold(row * A_DEV, total)

    @pl.when(at_start)
    def _():
        tail_copy.wait()
        early_rows(tail_ref)

    @pl.when(jnp.logical_not(at_start))
    def _():
        early_rows(samples_ref)

    out_copies = []
    low_lanes = lax.broadcasted_iota(jnp.int32, (ROWS, C_DEV), 1) < C_DEV // 2
    for q in range(CHUNKS):
        basis_copies[q].wait()
        even = jnp.dot(even_rows[...], basis_ref[q, 0], preferred_element_type=jnp.float32)
        odd = jnp.dot(odd_rows[...], basis_ref[q, 1], preferred_element_type=jnp.float32)
        for h in range(2):
            e = even[:, h * C_DEV : (h + 1) * C_DEV]
            o = odd[:, h * C_DEV : (h + 1) * C_DEV]
            real = jnp.where(low_lanes, e, pltpu.roll(o, C_DEV // 2, 1))
            imag = jnp.where(low_lanes, pltpu.roll(e, C_DEV // 2, 1), o)
            out_ref[2 * q + h, 0] = real.astype(jnp.bfloat16)
            out_ref[2 * q + h, 1] = imag.astype(jnp.bfloat16)
        copy = pltpu.make_async_copy(
            out_ref.at[pl.ds(2 * q, 2)], out_hbm.at[pl.ds(2 * q, 2)], out_sems.at[q]
        )
        copy.start()
        out_copies.append(copy)
    for copy in out_copies:
        copy.wait()


def channelize(place, samples, tail, taps, basis):
    anywhere = pl.BlockSpec(memory_space=pltpu.HBM)
    out = (PEERS, 2, ROWS, C_DEV)
    return pl.pallas_call(
        channelize_kernel,
        out_shape=jax.ShapeDtypeStruct(out, jnp.bfloat16),
        in_specs=[
            pl.BlockSpec(memory_space=pltpu.SMEM),
            anywhere,
            anywhere,
            pl.BlockSpec(memory_space=pltpu.VMEM),
            anywhere,
        ],
        out_specs=anywhere,
        scratch_shapes=[
            pltpu.VMEM(samples.shape, jnp.bfloat16),
            pltpu.VMEM(tail.shape, jnp.bfloat16),
            pltpu.VMEM(basis.shape, jnp.bfloat16),
            pltpu.VMEM((ROWS, L // 2), jnp.bfloat16),
            pltpu.VMEM((ROWS, L // 2), jnp.bfloat16),
            pltpu.VMEM(out, jnp.bfloat16),
            pltpu.SemaphoreType.DMA((2,)),
            pltpu.SemaphoreType.DMA((CHUNKS,)),
            pltpu.SemaphoreType.DMA((CHUNKS,)),
        ],
        compiler_params=pltpu.CompilerParams(vmem_limit_bytes=VMEM_WHOLE),
        name="channelize",
    )(place, samples, tail, taps, basis)


def joined(x_ref, ri, t):
    own = x_ref[t, ri, 0:OWN, :].astype(jnp.float32)
    early = x_ref[(t + 1) % PEERS, ri, OWN:ROWS, :].astype(jnp.float32)
    return own[:A_DEV], own[A_DEV:] + early


def lane_groups(shape):
    return lax.broadcasted_iota(jnp.int32, shape, len(shape) - 1) // GROUP


def pack_kernel(place_ref, x_ref, w_ref, rows, turned):
    shift = place_ref[0]
    group = lane_groups((A_DEV, C_DEV))
    for ri in range(2):
        for t in range(PEERS):
            k = ri * PEERS + t
            first, rest = joined(x_ref, ri, t)
            by_row = [first] + [rest[j * A_DEV : (j + 1) * A_DEV] for j in range(S_DEV - 1)]
            rolled = [
                [by_row[j]] + [pltpu.roll(by_row[j], m * GROUP, 1) for m in range(1, SPAN)]
                for j in range(S_DEV)
            ]
            for c4 in range(SPAN):
                merged = rolled[0][(0 - c4) % SPAN]
                for j in range(1, S_DEV):
                    merged = jnp.where(group == j, rolled[j][(j - c4) % SPAN], merged)
                start = pl.multiple_of(lax.rem(shift + c4, SPAN) * A_DEV, A_DEV)
                rows[k, pl.ds(start, A_DEV), :] = merged
    for k in range(2 * PEERS):
        turned[k * C_DEV : (k + 1) * C_DEV, :] = rows[k].T

    def step(cq, carry):
        w_ref[cq] = turned[pl.ds(cq, K, stride=GROUP), :].astype(jnp.bfloat16)
        return carry

    lax.fori_loop(0, GROUP, step, 0, unroll=8)


def pack(place, received):
    return pl.pallas_call(
        pack_kernel,
        out_shape=jax.ShapeDtypeStruct((GROUP, K, SPAN * A_DEV), jnp.bfloat16),
        in_specs=[pl.BlockSpec(memory_space=pltpu.SMEM), pl.BlockSpec(memory_space=pltpu.VMEM)],
        out_specs=pl.BlockSpec(memory_space=pltpu.VMEM),
        scratch_shapes=[
            pltpu.VMEM((2 * PEERS, OWN, C_DEV), jnp.float32),
            pltpu.VMEM((2 * PEERS * OWN, C_DEV), jnp.float32),
        ],
        compiler_params=pltpu.CompilerParams(vmem_limit_bytes=VMEM_LIMIT),
        name="pack",
    )(place, received)


def left_kernel(x_ref, left_ref, rows, turned):
    scale = 1.0 / (PEERS * S_DEV)
    for ri in range(2):
        for t in range(PEERS):
            start = (ri * PEERS + t) * OWN
            first, rest = joined(x_ref, ri, t)
            rows[start : start + A_DEV, :] = first * scale
            rows[start + A_DEV : start + OWN, :] = rest * scale
    for a in range(A_DEV):
        real = rows[pl.ds(a, K, stride=A_DEV), :]
        turned[a * C_DEV : (a + 1) * C_DEV, :] = real.T

    def step(c, carry):
        left_ref[c] = turned[pl.ds(c, A_DEV, stride=C_DEV), :].astype(jnp.bfloat16)
        return carry

    lax.fori_loop(0, C_DEV, step, 0, unroll=8)


def left_side(received):
    return pl.pallas_call(
        left_kernel,
        out_shape=jax.ShapeDtypeStruct((C_DEV, A_DEV, K), jnp.bfloat16),
        in_specs=[pl.BlockSpec(memory_space=pltpu.VMEM)],
        out_specs=pl.BlockSpec(memory_space=pltpu.VMEM),
        scratch_shapes=[
            pltpu.VMEM((2 * PEERS * OWN, C_DEV), jnp.float32),
            pltpu.VMEM((A_DEV * C_DEV, K), jnp.float32),
        ],
        compiler_params=pltpu.CompilerParams(vmem_limit_bytes=VMEM_LIMIT),
        cost_estimate=pl.CostEstimate(flops=0, bytes_accessed=64 << 20, transcendentals=0),
        name="left_side",
    )(received)


I_STEP = 8


def correlate_kernel(
    place_ref, table_ref, left_ref, own, core, cross, cross_w, swap, swap_w, far, far_w,
    out_ref, slots, products, sems,
):
    shift = place_ref[0]

    @pl.when(pl.program_id(0) == 0)
    def _():
        where = place_ref[2]
        late = where >= HALF - 2
        odd = lax.rem(where, 2) == 1
        before = where == HALF - 3

        def bring(e, condition, source):
            @pl.when(condition)
            def _():
                pltpu.make_async_copy(
                    source, slots.at[lax.rem(shift + e, SPAN)], sems.at[e]
                ).start()

        both, neither = jnp.logical_and, jnp.logical_not
        bring(0, where >= 0, own)
        bring(1, neither(odd), core)
        bring(1, both(odd, neither(late)), cross)
        bring(1, both(odd, late), cross_w)
        bring(2, neither(late), swap)
        bring(2, late, swap_w)
        bring(3, both(neither(odd), neither(late)), cross)
        bring(3, both(neither(odd), late), cross_w)
        bring(3, both(odd, neither(late | before)), far)
        bring(3, before, far_w)
        bring(3, both(odd, late), core)
        for e in range(SPAN):
            pltpu.make_async_copy(own, slots.at[lax.rem(shift + e, SPAN)], sems.at[e]).wait()
        group = lane_groups((K, SPAN * A_DEV))

        def step(cq, carry):
            held = [slots[b, cq] for b in range(SPAN)]
            for c4 in range(SPAN):
                right = held[(0 - c4) % SPAN]
                for p in range(1, SPAN):
                    right = jnp.where(group == p, held[(p - c4) % SPAN], right)
                lane = c4 * GROUP + cq
                channel = 2 * lax.rem(lane, C_DEV // 2) + c4 // 2
                crossed = jnp.concatenate([-right[K // 2 :], right[: K // 2]], axis=0)
                start = pl.multiple_of(channel * A_DEV, A_DEV)
                product = jnp.dot(
                    left_ref[lane],
                    jnp.concatenate([right, crossed], axis=1),
                    preferred_element_type=jnp.float32,
                )
                products[pl.ds(start, A_DEV), :] = product[:, : SPAN * A_DEV]
                products[pl.ds(C_DEV * A_DEV + start, A_DEV), :] = product[:, SPAN * A_DEV :]
            return carry

        lax.fori_loop(0, GROUP, step, 0, unroll=8)

    places = []
    for b in range(SPAN):
        offset = lax.rem(b - shift + SPAN, SPAN)
        position = jnp.int32(0)
        for tile in range(1, SPAN):
            position = position + jnp.where(table_ref[0, tile] == offset, tile, 0)
        places.append(position)
    channel = lax.broadcasted_iota(jnp.int32, (A_DEV, C_DEV), 1)
    group = 2 * (channel % 2) + channel // (C_DEV // 2)
    base = pl.program_id(0) * I_STEP
    for part in range(2):
        for i in range(I_STEP):
            row = part * C_DEV * A_DEV + base + i
            turned = products[pl.ds(row, C_DEV, stride=A_DEV), :].T
            pieces = [turned[p * A_DEV : (p + 1) * A_DEV] for p in range(SPAN)]
            for b in range(SPAN):
                tile = pieces[b]
                for c4 in range(1, SPAN):
                    tile = jnp.where(group == c4, pieces[(b + c4) % SPAN], tile)
                out_ref[0, places[b], part, i] = tile


def correlate(place, table, left, blocks):
    return pl.pallas_call(
        correlate_kernel,
        grid=(A_DEV // I_STEP,),
        out_shape=jax.ShapeDtypeStruct((1, SPAN, 2, A_DEV, A_DEV, C_DEV), jnp.float32),
        in_specs=[
            pl.BlockSpec(memory_space=pltpu.SMEM),
            pl.BlockSpec(memory_space=pltpu.SMEM),
            pl.BlockSpec(memory_space=pltpu.VMEM),
        ]
        + [pl.BlockSpec(memory_space=pltpu.HBM)] * len(blocks),
        out_specs=pl.BlockSpec(
            (1, SPAN, 2, I_STEP, A_DEV, C_DEV), lambda i: (0, 0, 0, i, 0, 0)
        ),
        scratch_shapes=[
            pltpu.VMEM((SPAN, GROUP, K, SPAN * A_DEV), jnp.bfloat16),
            pltpu.VMEM((2 * C_DEV * A_DEV, SPAN * A_DEV), jnp.float32),
            pltpu.SemaphoreType.DMA((SPAN,)),
        ],
        compiler_params=pltpu.CompilerParams(vmem_limit_bytes=VMEM_LIMIT),
        name="correlate",
    )(place, table, left, *blocks)


def send(block, pairs):
    return lax.ppermute(block, "inp", pairs)


def late(d):
    return d % HALF >= HALF - 2


def partners(own, received):
    count = lax.axis_size("inp")
    every = range(count)
    over = [((d + (1 if d % 2 else 3)) % count, d) for d in every]
    cross = send(own, [(s, d) for s, d in over if not late(d)])
    third = [((d + 3) % count, d) for d in every if d % 2 and late(d)]
    core = send(own, [(d + 1, d) for d in every if d % 2 == 0] + third)
    cross_w = send(own, [(s, d) for s, d in over if late(d)])
    received, _ = lax.optimization_barrier((received, own))
    cross, left = lax.optimization_barrier((cross, left_side(received)))
    ahead = [(d + 2, d) for d in every if d % 2 and not late(d)]
    far = send(cross, [(s, d) for s, d in ahead if not late(s)])
    swap = send(cross, [(d ^ 1, d) for d in every if not late(d)])
    far_w = send(cross_w, [(s, d) for s, d in ahead if late(s)])
    passed_w, far = lax.optimization_barrier((cross_w, far))
    swap_w = send(passed_w, [(d ^ 1, d) for d in every if late(d)])
    return left, [own, core, cross, passed_w, swap, swap_w, far, far_w]


def body(samples, tail, taps, tile_table):
    block = lax.axis_index("inp")
    place = jnp.stack([block % SPAN, lax.axis_index("tm"), block % HALF]).astype(jnp.int32)
    partial = channelize(place, samples, tail, taps, dft_basis())
    received = lax.all_to_all(partial, "tm", split_axis=0, concat_axis=0, tiled=True)
    own = pack(place, received)
    left, blocks = partners(own, received)
    return correlate(place, tile_table, left, blocks)


def solution(mesh):
    in_specs = (P("inp", "tm"), P("inp", None), P(), P("inp", None))
    out_specs = P("inp", None, None, None, None, "tm")
    return jax.shard_map(body, mesh=mesh, in_specs=in_specs, out_specs=out_specs, check_vma=False)
```

```python
import functools
import math

import jax
import jax.numpy as jnp
import numpy as np
from jax import lax
from jax.experimental import pallas as pl
from jax.experimental.pallas import tpu as pltpu
from jax.sharding import PartitionSpec as P

F = 1024
L = 2048
TAPS = 4
A_DEV = 32
S_DEV = 4
SPAN = 4
PEERS = 8
C_DEV = F // PEERS
CHUNKS = PEERS // 2
GROUP = 32
HALF = 32
OWN = S_DEV * A_DEV
EARLY = (TAPS - 1) * A_DEV
ROWS = OWN + EARLY
K = 2 * PEERS * S_DEV
VMEM_LIMIT = 24 * 1024 * 1024
VMEM_WHOLE = 62 * 1024 * 1024


def dft_basis():
    half = L // 2
    sample_rows = np.arange(half, dtype=np.int64)[:, None]
    channel_cols = np.arange(F, dtype=np.int64)[None, :]
    phase_index = sample_rows * channel_cols % L
    table_angles = np.arange(L, dtype=np.float32) * np.float32(2.0 * math.pi / L)
    norm_factor = np.float32(1.0 / math.sqrt(L))
    cosine_table = np.cos(table_angles).astype(np.float32) * norm_factor
    sine_table = -np.sin(table_angles).astype(np.float32) * norm_factor
    split = (half, CHUNKS, 2, C_DEV // 2, 2)
    cosines = cosine_table[phase_index].reshape(split)
    sines = sine_table[phase_index].reshape(split)
    whole_table = np.stack([cosines, sines], axis=3).transpose(1, 5, 0, 2, 3, 4)
    return jnp.asarray(whole_table.reshape(CHUNKS, 2, half, 4 * (C_DEV // 2)), dtype=jnp.bfloat16)


def channelize_kernel(
    samples_hbm, tail_hbm, taps_ref, basis_hbm, out_hbm,
    samples_ref, tail_ref, basis_ref, even_rows, odd_rows, out_ref, in_sems, basis_sems, out_sems,
):
    half = L // 2
    at_start = lax.axis_index("tm") == 0
    samples_copy = pltpu.make_async_copy(samples_hbm, samples_ref, in_sems.at[0])
    tail_copy = pltpu.make_async_copy(tail_hbm, tail_ref, in_sems.at[1])
    basis_copies = [
        pltpu.make_async_copy(basis_hbm.at[q], basis_ref.at[q], basis_sems.at[q])
        for q in range(CHUNKS)
    ]
    samples_copy.start()

    @pl.when(at_start)
    def _():
        tail_copy.start()

    for copy in basis_copies:
        copy.start()

    def frame(ref, index):
        return ref[:, index * L : (index + 1) * L].astype(jnp.float32)

    def tap(index):
        return taps_ref[index : index + 1, :]

    def fold(start, total):
        low, high = total[:, :half], total[:, half:]
        even_rows[start : start + A_DEV, :] = (low + high).astype(jnp.bfloat16)
        odd_rows[start : start + A_DEV, :] = (low - high).astype(jnp.bfloat16)

    def early_rows(ref):
        for row in range(TAPS - 1):
            total = tap(TAPS - 1) * frame(ref, row)
            for back in range(row):
                total = total + tap(TAPS - 1 - row + back) * frame(ref, back)
            fold(OWN + row * A_DEV, total)

    samples_copy.wait()
    for row in range(S_DEV):
        total = tap(0) * frame(samples_ref, row)
        for ahead in range(1, S_DEV - row):
            total = total + tap(ahead) * frame(samples_ref, row + ahead)
        fold(row * A_DEV, total)

    @pl.when(at_start)
    def _():
        tail_copy.wait()
        early_rows(tail_ref)

    @pl.when(jnp.logical_not(at_start))
    def _():
        early_rows(samples_ref)

    out_copies = []
    low_lanes = lax.broadcasted_iota(jnp.int32, (ROWS, C_DEV), 1) < C_DEV // 2
    for q in range(CHUNKS):
        basis_copies[q].wait()
        even = jnp.dot(even_rows[...], basis_ref[q, 0], preferred_element_type=jnp.float32)
        odd = jnp.dot(odd_rows[...], basis_ref[q, 1], preferred_element_type=jnp.float32)
        for h in range(2):
            e = even[:, h * C_DEV : (h + 1) * C_DEV]
            o = odd[:, h * C_DEV : (h + 1) * C_DEV]
            real = jnp.where(low_lanes, e, pltpu.roll(o, C_DEV // 2, 1))
            imag = jnp.where(low_lanes, pltpu.roll(e, C_DEV // 2, 1), o)
            out_ref[2 * q + h, 0] = real.astype(jnp.bfloat16)
            out_ref[2 * q + h, 1] = imag.astype(jnp.bfloat16)
        copy = pltpu.make_async_copy(
            out_ref.at[pl.ds(2 * q, 2)], out_hbm.at[pl.ds(2 * q, 2)], out_sems.at[q]
        )
        copy.start()
        out_copies.append(copy)
    for copy in out_copies:
        copy.wait()


def channelize(samples, tail, taps, basis):
    anywhere = pl.BlockSpec(memory_space=pltpu.HBM)
    out = (PEERS, 2, ROWS, C_DEV)
    return pl.pallas_call(
        channelize_kernel,
        out_shape=jax.ShapeDtypeStruct(out, jnp.bfloat16),
        in_specs=[
            anywhere,
            anywhere,
            pl.BlockSpec(memory_space=pltpu.VMEM),
            anywhere,
        ],
        out_specs=anywhere,
        scratch_shapes=[
            pltpu.VMEM(samples.shape, jnp.bfloat16),
            pltpu.VMEM(tail.shape, jnp.bfloat16),
            pltpu.VMEM(basis.shape, jnp.bfloat16),
            pltpu.VMEM((ROWS, L // 2), jnp.bfloat16),
            pltpu.VMEM((ROWS, L // 2), jnp.bfloat16),
            pltpu.VMEM(out, jnp.bfloat16),
            pltpu.SemaphoreType.DMA((2,)),
            pltpu.SemaphoreType.DMA((CHUNKS,)),
            pltpu.SemaphoreType.DMA((CHUNKS,)),
        ],
        compiler_params=pltpu.CompilerParams(vmem_limit_bytes=VMEM_WHOLE),
        name="channelize",
    )(samples, tail, taps, basis)


def joined(x_ref, ri, t):
    own = x_ref[t, ri, 0:OWN, :].astype(jnp.float32)
    early = x_ref[(t + 1) % PEERS, ri, OWN:ROWS, :].astype(jnp.float32)
    return own[:A_DEV], own[A_DEV:] + early


def lane_groups(shape):
    return lax.broadcasted_iota(jnp.int32, shape, len(shape) - 1) // GROUP


def pack_kernel(x_ref, w_ref, rows, turned):
    shift = lax.rem(lax.axis_index("inp"), SPAN)
    group = lane_groups((A_DEV, C_DEV))
    for ri in range(2):
        for t in range(PEERS):
            k = ri * PEERS + t
            first, rest = joined(x_ref, ri, t)
            by_row = [first] + [rest[j * A_DEV : (j + 1) * A_DEV] for j in range(S_DEV - 1)]
            rolled = [
                [by_row[j]] + [pltpu.roll(by_row[j], m * GROUP, 1) for m in range(1, SPAN)]
                for j in range(S_DEV)
            ]
            for c4 in range(SPAN):
                merged = rolled[0][(0 - c4) % SPAN]
                for j in range(1, S_DEV):
                    merged = jnp.where(group == j, rolled[j][(j - c4) % SPAN], merged)
                start = pl.multiple_of(lax.rem(shift + c4, SPAN) * A_DEV, A_DEV)
                rows[k, pl.ds(start, A_DEV), :] = merged
    for k in range(2 * PEERS):
        turned[k * C_DEV : (k + 1) * C_DEV, :] = rows[k].T

    def step(cq, carry):
        w_ref[cq] = turned[pl.ds(cq, K, stride=GROUP), :].astype(jnp.bfloat16)
        return carry

    lax.fori_loop(0, GROUP, step, 0, unroll=32)


def pack(received):
    return pl.pallas_call(
        pack_kernel,
        out_shape=jax.ShapeDtypeStruct((GROUP, K, SPAN * A_DEV), jnp.bfloat16),
        in_specs=[pl.BlockSpec(memory_space=pltpu.VMEM)],
        out_specs=pl.BlockSpec(memory_space=pltpu.VMEM),
        scratch_shapes=[
            pltpu.VMEM((2 * PEERS, OWN, C_DEV), jnp.float32),
            pltpu.VMEM((2 * PEERS * OWN, C_DEV), jnp.float32),
        ],
        compiler_params=pltpu.CompilerParams(vmem_limit_bytes=VMEM_LIMIT),
        name="pack",
    )(received)


def left_kernel(x_ref, left_ref, rows, turned):
    scale = 1.0 / (PEERS * S_DEV)
    for ri in range(2):
        for t in range(PEERS):
            start = (ri * PEERS + t) * OWN
            first, rest = joined(x_ref, ri, t)
            rows[start : start + A_DEV, :] = first * scale
            rows[start + A_DEV : start + OWN, :] = rest * scale
    for a in range(A_DEV):
        real = rows[pl.ds(a, K, stride=A_DEV), :]
        turned[a * C_DEV : (a + 1) * C_DEV, :] = real.T

    def step(c, carry):
        left_ref[c] = turned[pl.ds(c, A_DEV, stride=C_DEV), :].astype(jnp.bfloat16)
        return carry

    lax.fori_loop(0, C_DEV, step, 0, unroll=8)


def left_side(received):
    return pl.pallas_call(
        left_kernel,
        out_shape=jax.ShapeDtypeStruct((C_DEV, A_DEV, K), jnp.bfloat16),
        in_specs=[pl.BlockSpec(memory_space=pltpu.VMEM)],
        out_specs=pl.BlockSpec(memory_space=pltpu.VMEM),
        scratch_shapes=[
            pltpu.VMEM((2 * PEERS * OWN, C_DEV), jnp.float32),
            pltpu.VMEM((A_DEV * C_DEV, K), jnp.float32),
        ],
        compiler_params=pltpu.CompilerParams(vmem_limit_bytes=VMEM_LIMIT),
        cost_estimate=pl.CostEstimate(flops=0, bytes_accessed=64 << 20, transcendentals=0),
        name="left_side",
    )(received)


I_STEP = 16


def correlate_kernel(
    table_ref, left_ref, own, core, cross, cross_w, swap, swap_w, far, far_w,
    out_ref, slots, products, sems,
):
    block = lax.axis_index("inp")
    shift = lax.rem(block, SPAN)

    @pl.when(pl.program_id(0) == 0)
    def _():
        where = lax.rem(block, HALF)
        late = where >= HALF - 2
        odd = lax.rem(where, 2) == 1
        before = where == HALF - 3

        def bring(e, condition, source):
            @pl.when(condition)
            def _():
                pltpu.make_async_copy(
                    source, slots.at[lax.rem(shift + e, SPAN)], sems.at[e]
                ).start()

        both, neither = jnp.logical_and, jnp.logical_not
        bring(0, where >= 0, own)
        bring(1, neither(odd), core)
        bring(1, both(odd, neither(late)), cross)
        bring(1, both(odd, late), cross_w)
        bring(2, neither(late), swap)
        bring(2, late, swap_w)
        bring(3, both(neither(odd), neither(late)), cross)
        bring(3, both(neither(odd), late), cross_w)
        bring(3, both(odd, neither(late | before)), far)
        bring(3, before, far_w)
        bring(3, both(odd, late), core)
        for e in range(SPAN):
            pltpu.make_async_copy(own, slots.at[lax.rem(shift + e, SPAN)], sems.at[e]).wait()
        group = lane_groups((K, SPAN * A_DEV))

        def step(cq, carry):
            held = [slots[b, cq] for b in range(SPAN)]
            for c4 in range(SPAN):
                right = held[(0 - c4) % SPAN]
                for p in range(1, SPAN):
                    right = jnp.where(group == p, held[(p - c4) % SPAN], right)
                lane = c4 * GROUP + cq
                channel = 2 * lax.rem(lane, C_DEV // 2) + c4 // 2
                crossed = jnp.concatenate([-right[K // 2 :], right[: K // 2]], axis=0)
                start = pl.multiple_of(channel * A_DEV, A_DEV)
                product = jnp.dot(
                    left_ref[lane],
                    jnp.concatenate([right, crossed], axis=1),
                    preferred_element_type=jnp.float32,
                )
                products[pl.ds(start, A_DEV), :] = product[:, : SPAN * A_DEV]
                products[pl.ds(C_DEV * A_DEV + start, A_DEV), :] = product[:, SPAN * A_DEV :]
            return carry

        lax.fori_loop(0, GROUP, step, 0, unroll=16)

    places = []
    for b in range(SPAN):
        offset = lax.rem(b - shift + SPAN, SPAN)
        position = jnp.int32(0)
        for tile in range(1, SPAN):
            position = position + jnp.where(table_ref[0, tile] == offset, tile, 0)
        places.append(position)
    channel = lax.broadcasted_iota(jnp.int32, (A_DEV, C_DEV), 1)
    group = 2 * (channel % 2) + channel // (C_DEV // 2)
    base = pl.program_id(0) * I_STEP
    for part in range(2):
        for i in range(I_STEP):
            row = part * C_DEV * A_DEV + base + i
            turned = products[pl.ds(row, C_DEV, stride=A_DEV), :].T
            pieces = [turned[p * A_DEV : (p + 1) * A_DEV] for p in range(SPAN)]
            for b in range(SPAN):
                tile = pieces[b]
                for c4 in range(1, SPAN):
                    tile = jnp.where(group == c4, pieces[(b + c4) % SPAN], tile)
                out_ref[0, places[b], part, i] = tile


def correlate(table, left, blocks):
    return pl.pallas_call(
        correlate_kernel,
        grid=(A_DEV // I_STEP,),
        out_shape=jax.ShapeDtypeStruct((1, SPAN, 2, A_DEV, A_DEV, C_DEV), jnp.float32),
        in_specs=[
            pl.BlockSpec(memory_space=pltpu.SMEM),
            pl.BlockSpec(memory_space=pltpu.VMEM),
        ]
        + [pl.BlockSpec(memory_space=pltpu.HBM)] * len(blocks),
        out_specs=pl.BlockSpec(
            (1, SPAN, 2, I_STEP, A_DEV, C_DEV), lambda i: (0, 0, 0, i, 0, 0)
        ),
        scratch_shapes=[
            pltpu.VMEM((SPAN, GROUP, K, SPAN * A_DEV), jnp.bfloat16),
            pltpu.VMEM((2 * C_DEV * A_DEV, SPAN * A_DEV), jnp.float32),
            pltpu.SemaphoreType.DMA((SPAN,)),
        ],
        compiler_params=pltpu.CompilerParams(vmem_limit_bytes=VMEM_LIMIT),
        name="correlate",
    )(table, left, *blocks)


def send(block, pairs):
    return lax.ppermute(block, "inp", pairs)


def late(d):
    return d % HALF >= HALF - 2


def partners(own, received):
    count = lax.axis_size("inp")
    every = range(count)
    over = [((d + (1 if d % 2 else 3)) % count, d) for d in every]
    cross = send(own, [(s, d) for s, d in over if not late(d)])
    third = [((d + 3) % count, d) for d in every if d % 2 and late(d)]
    core = send(own, [(d + 1, d) for d in every if d % 2 == 0] + third)
    cross_w = send(own, [(s, d) for s, d in over if late(d)])
    received, _ = lax.optimization_barrier((received, own))
    cross, left = lax.optimization_barrier((cross, left_side(received)))
    ahead = [(d + 2, d) for d in every if d % 2 and not late(d)]
    far = send(cross, [(s, d) for s, d in ahead if not late(s)])
    swap = send(cross, [(d ^ 1, d) for d in every if not late(d)])
    far_w = send(cross_w, [(s, d) for s, d in ahead if late(s)])
    passed_w, far = lax.optimization_barrier((cross_w, far))
    swap_w = send(passed_w, [(d ^ 1, d) for d in every if late(d)])
    return left, [own, core, cross, passed_w, swap, swap_w, far, far_w]


def body(samples, tail, taps, tile_table):
    partial = channelize(samples, tail, taps, dft_basis())
    received = lax.all_to_all(partial, "tm", split_axis=0, concat_axis=0, tiled=True)
    own = pack(received)
    left, blocks = partners(own, received)
    return correlate(tile_table, left, blocks)


def solution(mesh):
    in_specs = (P("inp", "tm"), P("inp", None), P(), P("inp", None))
    out_specs = P("inp", None, None, None, None, "tm")
    return jax.shard_map(body, mesh=mesh, in_specs=in_specs, out_specs=out_specs, check_vma=False)
```

```python
import functools
import math

import jax
import jax.numpy as jnp
import numpy as np
from jax import lax
from jax.experimental import pallas as pl
from jax.experimental.pallas import tpu as pltpu
from jax.sharding import PartitionSpec as P

F = 1024
L = 2048
TAPS = 4
A_DEV = 32
S_DEV = 4
SPAN = 4
PEERS = 8
C_DEV = F // PEERS
CHUNKS = PEERS // 2
GROUP = 32
HALF = 32
OWN = S_DEV * A_DEV
EARLY = (TAPS - 1) * A_DEV
ROWS = OWN + EARLY
K = 2 * PEERS * S_DEV
VMEM_LIMIT = 24 * 1024 * 1024
VMEM_WHOLE = 62 * 1024 * 1024


def dft_basis():
    half = L // 2
    sample_rows = np.arange(half, dtype=np.int64)[:, None]
    channel_cols = np.arange(F, dtype=np.int64)[None, :]
    phase_index = sample_rows * channel_cols % L
    table_angles = np.arange(L, dtype=np.float32) * np.float32(2.0 * math.pi / L)
    norm_factor = np.float32(1.0 / math.sqrt(L))
    cosine_table = np.cos(table_angles).astype(np.float32) * norm_factor
    sine_table = -np.sin(table_angles).astype(np.float32) * norm_factor
    split = (half, CHUNKS, 2, C_DEV // 2, 2)
    cosines = cosine_table[phase_index].reshape(split)
    sines = sine_table[phase_index].reshape(split)
    whole_table = np.stack([cosines, sines], axis=3).transpose(1, 5, 0, 2, 3, 4)
    return jnp.asarray(whole_table.reshape(CHUNKS, 2, half, 4 * (C_DEV // 2)), dtype=jnp.bfloat16)


def channelize_kernel(
    samples_hbm, tail_hbm, taps_ref, basis_hbm, out_hbm,
    samples_ref, tail_ref, basis_ref, even_rows, odd_rows, out_ref, in_sems, basis_sems, out_sems,
):
    half = L // 2
    at_start = lax.axis_index("tm") == 0
    samples_copy = pltpu.make_async_copy(samples_hbm, samples_ref, in_sems.at[0])
    tail_copy = pltpu.make_async_copy(tail_hbm, tail_ref, in_sems.at[1])
    basis_copies = [
        pltpu.make_async_copy(basis_hbm.at[q], basis_ref.at[q], basis_sems.at[q])
        for q in range(CHUNKS)
    ]
    samples_copy.start()

    @pl.when(at_start)
    def _():
        tail_copy.start()

    basis_copies[0].start()

    def frame(ref, index):
        return ref[:, index * L : (index + 1) * L].astype(jnp.float32)

    def tap(index):
        return taps_ref[index : index + 1, :]

    def fold(start, total):
        low, high = total[:, :half], total[:, half:]
        even_rows[start : start + A_DEV, :] = (low + high).astype(jnp.bfloat16)
        odd_rows[start : start + A_DEV, :] = (low - high).astype(jnp.bfloat16)

    def early_rows(ref):
        for row in range(TAPS - 1):
            total = tap(TAPS - 1) * frame(ref, row)
            for back in range(row):
                total = total + tap(TAPS - 1 - row + back) * frame(ref, back)
            fold(OWN + row * A_DEV, total)

    samples_copy.wait()
    for copy in basis_copies[1:]:
        copy.start()
    for row in range(S_DEV):
        total = tap(0) * frame(samples_ref, row)
        for ahead in range(1, S_DEV - row):
            total = total + tap(ahead) * frame(samples_ref, row + ahead)
        fold(row * A_DEV, total)

    @pl.when(at_start)
    def _():
        tail_copy.wait()
        early_rows(tail_ref)

    @pl.when(jnp.logical_not(at_start))
    def _():
        early_rows(samples_ref)

    out_copies = []
    low_lanes = lax.broadcasted_iota(jnp.int32, (ROWS, C_DEV), 1) < C_DEV // 2
    for q in range(CHUNKS):
        basis_copies[q].wait()
        even = jnp.dot(even_rows[...], basis_ref[q, 0], preferred_element_type=jnp.float32)
        odd = jnp.dot(odd_rows[...], basis_ref[q, 1], preferred_element_type=jnp.float32)
        for h in range(2):
            e = even[:, h * C_DEV : (h + 1) * C_DEV]
            o = odd[:, h * C_DEV : (h + 1) * C_DEV]
            real = jnp.where(low_lanes, e, pltpu.roll(o, C_DEV // 2, 1))
            imag = jnp.where(low_lanes, pltpu.roll(e, C_DEV // 2, 1), o)
            out_ref[2 * q + h, 0] = real.astype(jnp.bfloat16)
            out_ref[2 * q + h, 1] = imag.astype(jnp.bfloat16)
        copy = pltpu.make_async_copy(
            out_ref.at[pl.ds(2 * q, 2)], out_hbm.at[pl.ds(2 * q, 2)], out_sems.at[q]
        )
        copy.start()
        out_copies.append(copy)
    for copy in out_copies:
        copy.wait()


def channelize(samples, tail, taps, basis):
    anywhere = pl.BlockSpec(memory_space=pltpu.HBM)
    out = (PEERS, 2, ROWS, C_DEV)
    return pl.pallas_call(
        channelize_kernel,
        out_shape=jax.ShapeDtypeStruct(out, jnp.bfloat16),
        in_specs=[
            anywhere,
            anywhere,
            pl.BlockSpec(memory_space=pltpu.VMEM),
            anywhere,
        ],
        out_specs=anywhere,
        scratch_shapes=[
            pltpu.VMEM(samples.shape, jnp.bfloat16),
            pltpu.VMEM(tail.shape, jnp.bfloat16),
            pltpu.VMEM(basis.shape, jnp.bfloat16),
            pltpu.VMEM((ROWS, L // 2), jnp.bfloat16),
            pltpu.VMEM((ROWS, L // 2), jnp.bfloat16),
            pltpu.VMEM(out, jnp.bfloat16),
            pltpu.SemaphoreType.DMA((2,)),
            pltpu.SemaphoreType.DMA((CHUNKS,)),
            pltpu.SemaphoreType.DMA((CHUNKS,)),
        ],
        compiler_params=pltpu.CompilerParams(vmem_limit_bytes=VMEM_WHOLE),
        name="channelize",
    )(samples, tail, taps, basis)


def joined(x_ref, ri, t):
    own = x_ref[t, ri, 0:OWN, :].astype(jnp.float32)
    early = x_ref[(t + 1) % PEERS, ri, OWN:ROWS, :].astype(jnp.float32)
    return own[:A_DEV], own[A_DEV:] + early


def lane_groups(shape):
    return lax.broadcasted_iota(jnp.int32, shape, len(shape) - 1) // GROUP


def pack_kernel(x_ref, w_ref, rows, turned):
    shift = lax.rem(lax.axis_index("inp"), SPAN)
    group = lane_groups((A_DEV, C_DEV))
    for ri in range(2):
        for t in range(PEERS):
            k = ri * PEERS + t
            first, rest = joined(x_ref, ri, t)
            by_row = [first] + [rest[j * A_DEV : (j + 1) * A_DEV] for j in range(S_DEV - 1)]
            rolled = [
                [by_row[j]] + [pltpu.roll(by_row[j], m * GROUP, 1) for m in range(1, SPAN)]
                for j in range(S_DEV)
            ]
            for c4 in range(SPAN):
                merged = rolled[0][(0 - c4) % SPAN]
                for j in range(1, S_DEV):
                    merged = jnp.where(group == j, rolled[j][(j - c4) % SPAN], merged)
                start = pl.multiple_of(lax.rem(shift + c4, SPAN) * A_DEV, A_DEV)
                rows[k, pl.ds(start, A_DEV), :] = merged
    for k in range(2 * PEERS):
        turned[k * C_DEV : (k + 1) * C_DEV, :] = rows[k].T

    def step(cq, carry):
        w_ref[cq] = turned[pl.ds(cq, K, stride=GROUP), :].astype(jnp.bfloat16)
        return carry

    lax.fori_loop(0, GROUP, step, 0, unroll=32)


def pack(received):
    return pl.pallas_call(
        pack_kernel,
        out_shape=jax.ShapeDtypeStruct((GROUP, K, SPAN * A_DEV), jnp.bfloat16),
        in_specs=[pl.BlockSpec(memory_space=pltpu.VMEM)],
        out_specs=pl.BlockSpec(memory_space=pltpu.VMEM),
        scratch_shapes=[
            pltpu.VMEM((2 * PEERS, OWN, C_DEV), jnp.float32),
            pltpu.VMEM((2 * PEERS * OWN, C_DEV), jnp.float32),
        ],
        compiler_params=pltpu.CompilerParams(vmem_limit_bytes=VMEM_LIMIT),
        name="pack",
    )(received)


def left_kernel(x_ref, left_ref, rows, turned):
    scale = 1.0 / (PEERS * S_DEV)
    for ri in range(2):
        for t in range(PEERS):
            start = (ri * PEERS + t) * OWN
            first, rest = joined(x_ref, ri, t)
            rows[start : start + A_DEV, :] = first * scale
            rows[start + A_DEV : start + OWN, :] = rest * scale
    for a in range(A_DEV):
        real = rows[pl.ds(a, K, stride=A_DEV), :]
        turned[a * C_DEV : (a + 1) * C_DEV, :] = real.T

    def step(c, carry):
        left_ref[c] = turned[pl.ds(c, A_DEV, stride=C_DEV), :].astype(jnp.bfloat16)
        return carry

    lax.fori_loop(0, C_DEV, step, 0, unroll=32)


def left_side(received):
    return pl.pallas_call(
        left_kernel,
        out_shape=jax.ShapeDtypeStruct((C_DEV, A_DEV, K), jnp.bfloat16),
        in_specs=[pl.BlockSpec(memory_space=pltpu.VMEM)],
        out_specs=pl.BlockSpec(memory_space=pltpu.VMEM),
        scratch_shapes=[
            pltpu.VMEM((2 * PEERS * OWN, C_DEV), jnp.float32),
            pltpu.VMEM((A_DEV * C_DEV, K), jnp.float32),
        ],
        compiler_params=pltpu.CompilerParams(vmem_limit_bytes=VMEM_LIMIT),
        cost_estimate=pl.CostEstimate(flops=0, bytes_accessed=64 << 20, transcendentals=0),
        name="left_side",
    )(received)


I_STEP = 16


def correlate_kernel(
    table_ref, left_ref, own, core, cross, cross_w, swap, swap_w, far, far_w,
    out_ref, slots, products, sems,
):
    block = lax.axis_index("inp")
    shift = lax.rem(block, SPAN)

    @pl.when(pl.program_id(0) == 0)
    def _():
        where = lax.rem(block, HALF)
        late = where >= HALF - 2
        odd = lax.rem(where, 2) == 1
        before = where == HALF - 3

        def bring(e, condition, source):
            @pl.when(condition)
            def _():
                pltpu.make_async_copy(
                    source, slots.at[lax.rem(shift + e, SPAN)], sems.at[e]
                ).start()

        both, neither = jnp.logical_and, jnp.logical_not
        bring(0, where >= 0, own)
        bring(1, neither(odd), core)
        bring(1, both(odd, neither(late)), cross)
        bring(1, both(odd, late), cross_w)
        bring(2, neither(late), swap)
        bring(2, late, swap_w)
        bring(3, both(neither(odd), neither(late)), cross)
        bring(3, both(neither(odd), late), cross_w)
        bring(3, both(odd, neither(late | before)), far)
        bring(3, before, far_w)
        bring(3, both(odd, late), core)
        for e in range(SPAN):
            pltpu.make_async_copy(own, slots.at[lax.rem(shift + e, SPAN)], sems.at[e]).wait()
        group = lane_groups((K, SPAN * A_DEV))

        def step(cq, carry):
            held = [slots[b, cq] for b in range(SPAN)]
            for c4 in range(SPAN):
                right = held[(0 - c4) % SPAN]
                for p in range(1, SPAN):
                    right = jnp.where(group == p, held[(p - c4) % SPAN], right)
                lane = c4 * GROUP + cq
                channel = 2 * lax.rem(lane, C_DEV // 2) + c4 // 2
                crossed = jnp.concatenate([-right[K // 2 :], right[: K // 2]], axis=0)
                start = pl.multiple_of(channel * A_DEV, A_DEV)
                product = jnp.dot(
                    left_ref[lane],
                    jnp.concatenate([right, crossed], axis=1),
                    preferred_element_type=jnp.float32,
                )
                products[pl.ds(start, A_DEV), :] = product[:, : SPAN * A_DEV]
                products[pl.ds(C_DEV * A_DEV + start, A_DEV), :] = product[:, SPAN * A_DEV :]
            return carry

        lax.fori_loop(0, GROUP, step, 0, unroll=16)

    places = []
    for b in range(SPAN):
        offset = lax.rem(b - shift + SPAN, SPAN)
        position = jnp.int32(0)
        for tile in range(1, SPAN):
            position = position + jnp.where(table_ref[0, tile] == offset, tile, 0)
        places.append(position)
    channel = lax.broadcasted_iota(jnp.int32, (A_DEV, C_DEV), 1)
    group = 2 * (channel % 2) + channel // (C_DEV // 2)
    base = pl.program_id(0) * I_STEP
    for part in range(2):
        for i in range(I_STEP):
            row = part * C_DEV * A_DEV + base + i
            turned = products[pl.ds(row, C_DEV, stride=A_DEV), :].T
            pieces = [turned[p * A_DEV : (p + 1) * A_DEV] for p in range(SPAN)]
            for b in range(SPAN):
                tile = pieces[b]
                for c4 in range(1, SPAN):
                    tile = jnp.where(group == c4, pieces[(b + c4) % SPAN], tile)
                out_ref[0, places[b], part, i] = tile


def correlate(table, left, blocks):
    return pl.pallas_call(
        correlate_kernel,
        grid=(A_DEV // I_STEP,),
        out_shape=jax.ShapeDtypeStruct((1, SPAN, 2, A_DEV, A_DEV, C_DEV), jnp.float32),
        in_specs=[
            pl.BlockSpec(memory_space=pltpu.SMEM),
            pl.BlockSpec(memory_space=pltpu.VMEM),
        ]
        + [pl.BlockSpec(memory_space=pltpu.HBM)] * len(blocks),
        out_specs=pl.BlockSpec(
            (1, SPAN, 2, I_STEP, A_DEV, C_DEV), lambda i: (0, 0, 0, i, 0, 0)
        ),
        scratch_shapes=[
            pltpu.VMEM((SPAN, GROUP, K, SPAN * A_DEV), jnp.bfloat16),
            pltpu.VMEM((2 * C_DEV * A_DEV, SPAN * A_DEV), jnp.float32),
            pltpu.SemaphoreType.DMA((SPAN,)),
        ],
        compiler_params=pltpu.CompilerParams(vmem_limit_bytes=VMEM_LIMIT),
        name="correlate",
    )(table, left, *blocks)


def send(block, pairs):
    return lax.ppermute(block, "inp", pairs)


def late(d):
    return d % HALF >= HALF - 2


def partners(own, received):
    count = lax.axis_size("inp")
    every = range(count)
    over = [((d + (1 if d % 2 else 3)) % count, d) for d in every]
    cross = send(own, [(s, d) for s, d in over if not late(d)])
    third = [((d + 3) % count, d) for d in every if d % 2 and late(d)]
    core = send(own, [(d + 1, d) for d in every if d % 2 == 0] + third)
    cross_w = send(own, [(s, d) for s, d in over if late(d)])
    received, _ = lax.optimization_barrier((received, own))
    cross, left = lax.optimization_barrier((cross, left_side(received)))
    ahead = [(d + 2, d) for d in every if d % 2 and not late(d)]
    far = send(cross, [(s, d) for s, d in ahead if not late(s)])
    swap = send(cross, [(d ^ 1, d) for d in every if not late(d)])
    far_w = send(cross_w, [(s, d) for s, d in ahead if late(s)])
    passed_w, far = lax.optimization_barrier((cross_w, far))
    swap_w = send(passed_w, [(d ^ 1, d) for d in every if late(d)])
    return left, [own, core, cross, passed_w, swap, swap_w, far, far_w]


def body(samples, tail, taps, tile_table):
    partial = channelize(samples, tail, taps, dft_basis())
    received = lax.all_to_all(partial, "tm", split_axis=0, concat_axis=0, tiled=True)
    own = pack(received)
    left, blocks = partners(own, received)
    return correlate(tile_table, left, blocks)


def solution(mesh):
    in_specs = (P("inp", "tm"), P("inp", None), P(), P("inp", None))
    out_specs = P("inp", None, None, None, None, "tm")
    return jax.shard_map(body, mesh=mesh, in_specs=in_specs, out_specs=out_specs, check_vma=False)
```
